32 devices in a mesh: tun: 8 (over y, x, core), sec: 4 (over z).
Axes of the slice: x: 2, y: 2, z: 4, core: 2. Of those that a mesh axis runs over, the one named last changes fastest.
Arguments:
- wind_vector: float32 [3, 64, 64, 128], P(None, 'tun', 'sec'), may hold values from -3 to 3
- thermal_surplus: float32 [64, 64, 128], P('tun', 'sec'), may hold values from -4 to 4
- carbon_particulate: float32 [64, 64, 128], P('tun', 'sec'), may hold values from 0 to 1
- particle_bin_weight: float32 [16, 64, 64, 128], P(None, 'tun', 'sec'), may hold values from 0 to 1
- particle_bin_tally: int32 [64, 64, 128], P('tun', 'sec'), may hold values from 0 to 16
- spray_region_label: int32 [64, 64, 128], P('tun', 'sec'), may hold values from 0 to 8
- nozzle_onset_step: int32 [8], replicated, may hold values from 0 to 2
Outputs:
- velocity_out: float32 [3, 64, 64, 128], P(None, 'tun', 'sec')
- temperature_out: float32 [64, 64, 128], P('tun', 'sec')
- soot_out: float32 [64, 64, 128], P('tun', 'sec')
- mass_out: float32 [16, 64, 64, 128], P(None, 'tun', 'sec')
- count_out: int32 [64, 64, 128], P('tun', 'sec')
The draws below stay inside these ranges and needn't reach their ends.
Inputs may be any that keep to these rules, and one draw needn't show every extreme that they name: A cell's live slots are its first particle_bin_tally slots.
All inputs are finite; a program needn't handle non-finite values.
Results may differ from the reference program's by a relative error of at most 0.0003.
Values sent between devices are 32-bit elements; how exact they have to be, the bound alone decides.
A program may use at most 64 MiB of HBM per device.

```python
import jax
import jax.numpy as jnp
from jax import lax

VERTICAL_EXTENT = 128
DS = 16
NZONE = 8
TUNNELWISE_SIZE = 64
LATERAL_EXTENT = 64


def set_ends(values, own_key, least, high):
    spot = [jax.random.randint(jax.random.fold_in(own_key, axis), (), 0, length) for axis, length in enumerate(values.shape)]
    main_axis = values.shape.index(max(values.shape))
    beside = spot[:main_axis] + [(spot[main_axis] + 1) % values.shape[main_axis]] + spot[main_axis + 1:]
    return values.at[tuple(spot)].set(least).at[tuple(beside)].set(high)


def level_of(stream_key, extent, shards, low, high):
    def one(position, parts):
        steps = jax.random.uniform(jax.random.fold_in(jax.random.fold_in(stream_key, 6), position), (parts,), jnp.float32, low / len(shards), high / len(shards))
        return jnp.repeat(jnp.exp(steps), extent[position] // parts).reshape((-1,) + (1,) * (len(extent) - position - 1))

    level = one(*shards[0])
    for cut in shards[1:]:
        level = level * one(*cut)
    return level


def gaussian(own_key, extent, deviation, reach, split=(), kind=jnp.bfloat16):
    values = deviation * jax.random.normal(own_key, extent, jnp.float32)
    if split:
        values = values * level_of(own_key, extent, split, -0.22, 0.18)
    return jnp.clip(values, -reach, reach).astype(kind)


def setup_inputs(seed: int = 0) -> dict:
    streams_of = jax.random.split(jax.random.key(seed), 8)
    wind_vector = gaussian(streams_of[0], (3, TUNNELWISE_SIZE, LATERAL_EXTENT, VERTICAL_EXTENT), 0.5, 3.0, ((1, 8), (2, 4)), jnp.float32)
    thermal_surplus = gaussian(streams_of[1], (TUNNELWISE_SIZE, LATERAL_EXTENT, VERTICAL_EXTENT), 1.0, 4.0, ((0, 8), (1, 4)), jnp.float32)
    carbon_particulate = jnp.clip(1.0 * jax.random.uniform(streams_of[2], (TUNNELWISE_SIZE, LATERAL_EXTENT, VERTICAL_EXTENT), jnp.float32) ** level_of(streams_of[2], (TUNNELWISE_SIZE, LATERAL_EXTENT, VERTICAL_EXTENT), ((0, 8), (1, 4)), -0.2, 0.2), 0.0, 1.0)
    particle_bin_weight = jnp.clip(1.0 * jax.random.uniform(streams_of[3], (DS, TUNNELWISE_SIZE, LATERAL_EXTENT, VERTICAL_EXTENT), jnp.float32) ** level_of(streams_of[3], (DS, TUNNELWISE_SIZE, LATERAL_EXTENT, VERTICAL_EXTENT), ((1, 8), (2, 4)), -0.2, 0.2), 0.0, 1.0)
    particle_bin_tally = set_ends(jax.random.randint(streams_of[4], (TUNNELWISE_SIZE, LATERAL_EXTENT, VERTICAL_EXTENT), 0, DS + 1), jax.random.fold_in(streams_of[4], 1), 0, DS).astype(jnp.int32)
    spray_region_label = set_ends(jax.random.randint(streams_of[5], (TUNNELWISE_SIZE, LATERAL_EXTENT, VERTICAL_EXTENT), 0, NZONE + 1), jax.random.fold_in(streams_of[5], 1), 0, NZONE).astype(jnp.int32)
    nozzle_onset_step = set_ends(jax.random.randint(streams_of[6], (NZONE,), 0, 3), jax.random.fold_in(streams_of[6], 1), 0, 2).astype(jnp.int32)
    return {"wind_vector": wind_vector, "thermal_surplus": thermal_surplus, "carbon_particulate": carbon_particulate, "particle_bin_weight": particle_bin_weight, "particle_bin_tally": particle_bin_tally, "spray_region_label": spray_region_label, "nozzle_onset_step": nozzle_onset_step}


visc_base = 0.2
time_step = 0.1
buoyancy = 0.5
drag_rate = 0.3
vent_speed = 1.0
inject_rate = 0.5
evap_rate = 0.4
latent_heat = 0.5
scavenge = 0.3


def neighbour(array, dim, offset):
    result = array
    lead = array.ndim - 3
    for split_axis in range(3):
        full = array.shape[lead + split_axis]
        start = 1 + offset if split_axis == dim else 1
        result = lax.slice_in_dim(result, start, start + full - 2, axis=lead + split_axis)
    return result


def advance(padded):
    centre = neighbour(padded, 0, 0)
    viscous = visc_base * (1.0 + 0.5 * jnp.tanh(padded[3]))
    visc_centre = neighbour(viscous, 0, 0)
    diffusion = jnp.zeros_like(centre)
    advection = jnp.zeros_like(centre)
    for dim in range(3):
        upper = neighbour(padded, dim, 1)
        lower = neighbour(padded, dim, -1)
        diffusion = diffusion + 0.5 * (visc_centre + neighbour(viscous, dim, 1)) * (upper - centre)
        diffusion = diffusion + 0.5 * (visc_centre + neighbour(viscous, dim, -1)) * (lower - centre)
        advection = advection + 0.5 * centre[dim] * (upper - lower)
    fresh = centre + time_step * (diffusion - advection)
    along = fresh[0] + time_step * drag_rate * (vent_speed - centre[0])
    upward = fresh[2] + time_step * buoyancy * centre[3]
    return jnp.stack([along, fresh[1], upward, fresh[3], fresh[4]])


def mist(transport_state, mass, count, spray_region_label, nozzle_onset_step, substep):
    slots = jnp.arange(mass.shape[0], dtype=jnp.int32)
    live = (slots[:, None, None, None] < count[None]).astype(jnp.float32)
    zones = jnp.arange(1, nozzle_onset_step.shape[0] + 1, dtype=jnp.int32)
    spraying = (nozzle_onset_step <= substep).astype(jnp.float32)
    zone_hit = (spray_region_label[None] == zones[:, None, None, None]).astype(jnp.float32)
    active = jnp.sum(zone_hit * spraying[:, None, None, None], axis=0)
    mass = mass + inject_rate * live * active[None]
    loaded = jnp.sum(live * mass, axis=0)
    evaporated = evap_rate * live * mass * jax.nn.sigmoid(transport_state[3])[None]
    heat = transport_state[3] - latent_heat * jnp.sum(evaporated, axis=0)
    sooty = transport_state[4] / (1.0 + scavenge * loaded)
    transport_state = jnp.stack([transport_state[0], transport_state[1], transport_state[2], heat, sooty])
    return transport_state, mass - evaporated


def reference(wind_vector, thermal_surplus, carbon_particulate, particle_bin_weight, particle_bin_tally, spray_region_label, nozzle_onset_step):
    transport_state = jnp.concatenate([wind_vector, thermal_surplus[None], carbon_particulate[None]], axis=0)
    mass, count = particle_bin_weight, particle_bin_tally
    for substep in range(2):
        padded = jnp.pad(transport_state, ((0, 0), (1, 1), (1, 1), (1, 1)))
        transport_state = advance(padded)
        mass = jnp.pad(mass, ((0, 0), (1, 0), (0, 0), (0, 0)))[:, :-1]
        count = jnp.pad(count, ((1, 0), (0, 0), (0, 0)))[:-1]
        transport_state, mass = mist(transport_state, mass, count, spray_region_label, nozzle_onset_step, substep)
    return transport_state[0:3], transport_state[3], transport_state[4], mass, count
```

```python
import functools

import jax
import jax.numpy as jnp
from jax import lax
from jax.experimental import pallas as pl
from jax.experimental.pallas import tpu as pltpu
from jax.sharding import PartitionSpec as P

visc_base = 0.2
time_step = 0.1
buoyancy = 0.5
drag_rate = 0.3
vent_speed = 1.0
inject_rate = 0.5
evap_rate = 0.4
latent_heat = 0.5
scavenge = 0.3

MESH = pl.DeviceIdType.MESH
FIELDS = 5
LOAD, TALLY, SPRAY = 5, 6, 7
ALL = 8


def shifted(c, lane):
    rows, depth = c.shape
    below = pltpu.roll(c, 1, 0)
    above = pltpu.roll(c, rows - 1, 0)
    down = jnp.where(lane == 0, 0.0, pltpu.roll(c, 1, 1))
    up = jnp.where(lane == depth - 1, 0.0, pltpu.roll(c, depth - 1, 1))
    return below, above, down, up


def transported(q, behind, ahead, th, th_behind, th_ahead, lane, keep):
    cut = lambda a: a[:keep]
    around_th = [cut(a) for a in shifted(th, lane)]
    th0 = cut(th)
    half = 0.5 * time_step
    base = 2.0 * visc_base * half
    slope = 0.5 * visc_base * half
    mine = base + slope * th0
    wind = [half * cut(q[d]) for d in range(3)]
    a = [mine + slope * t for t in [cut(th_behind), cut(th_ahead)] + around_th]
    weights = [
        a[0] + wind[0], a[1] - wind[0],
        a[2] + wind[1], a[3] - wind[1],
        a[4] + wind[2], a[5] - wind[2],
    ]
    own = 1.0 - ((a[0] + a[1]) + (a[2] + a[3]) + (a[4] + a[5]))
    fresh = []
    for f in range(FIELDS):
        near = [cut(behind[f]), cut(ahead[f])] + [cut(s) for s in shifted(q[f], lane)]
        terms = [w * n for w, n in zip(weights, near)]
        fresh.append(
            (own * cut(q[f]) + terms[0])
            + (terms[1] + terms[2])
            + (terms[3] + terms[4])
            + terms[5]
        )
    fresh[0] = fresh[0] + time_step * drag_rate * (vent_speed - cut(q[0]))
    fresh[2] = fresh[2] + time_step * buoyancy * cut(q[3])
    return fresh


def droplet(heat, soot, sprayed):
    kept = (1.0 - 0.5 * evap_rate) - 0.5 * evap_rate * jnp.tanh(0.5 * heat)
    heat = heat - latent_heat * (1.0 - kept) * sprayed
    soot = soot / (1.0 + scavenge * sprayed)
    return heat, soot, kept


def exchange_kernel(
    tun_size, sec_size,
    wind_hbm, heat_hbm, soot_hbm, mass_hbm, count_hbm, label_hbm, onset,
    state, coef, mass_in,
    ext, first, kept_first, spray_next, mass, count, label,
    pack_low, pack_high, from_low, from_high,
    local_sem, send_sem, recv_sem,
):
    X, Y, Z = heat_hbm.shape
    slots = mass_hbm.shape[0]
    t, s = lax.axis_index("tun"), lax.axis_index("sec")
    has = {-1: t > 0, 1: t < tun_size - 1}
    has_sec = {-1: s > 0, 1: s < sec_size - 1}

    def exists(dt, ds):
        if dt and ds:
            return jnp.logical_and(has[dt], has_sec[ds])
        return has[dt] if dt else has_sec[ds]

    around = [(a, b) for a in (-1, 0, 1) for b in (-1, 0, 1) if a or b]

    def load(i, src, dst):
        return pltpu.make_async_copy(src, dst, local_sem.at[i])

    loads = [
        load(0, count_hbm, count),
        load(1, label_hbm, label),
        load(2, mass_hbm, mass),
        load(3, wind_hbm, ext.at[0:3, 2:X + 2, 0:Y]),
        load(4, heat_hbm, ext.at[3, 2:X + 2, 0:Y]),
        load(5, soot_hbm, ext.at[4, 2:X + 2, 0:Y]),
    ]
    for c in loads:
        c.start()

    barrier = pltpu.get_barrier_semaphore()
    for a, b in around:
        @pl.when(exists(a, b))
        def _(a=a, b=b):
            pl.semaphore_signal(
                barrier, inc=1, device_id={"tun": t + a, "sec": s + b}, device_id_type=MESH
            )
    wide = has[-1].astype(jnp.int32) + has[1].astype(jnp.int32)
    deep = has_sec[-1].astype(jnp.int32) + has_sec[1].astype(jnp.int32)
    pl.semaphore_wait(barrier, (1 + wide) * (1 + deep) - 1)

    def send(i, a, b, src, dst):
        return (a, b, pltpu.make_async_remote_copy(
            src_ref=src, dst_ref=dst, send_sem=send_sem.at[i], recv_sem=recv_sem.at[i],
            device_id={"tun": t + a, "sec": s + b}, device_id_type=MESH,
        ))

    def start(group):
        for a, b, copy in group:
            @pl.when(exists(a, b))
            def _(copy=copy):
                copy.start()

    def wait_recv(group):
        for a, b, copy in group:
            @pl.when(exists(-a, -b))
            def _(copy=copy):
                copy.wait_recv()

    fields = [
        send(0, 1, 0, wind_hbm.at[:, X - 2:X], ext.at[0:3, 0:2, 0:Y]),
        send(1, 1, 0, heat_hbm.at[X - 2:X], ext.at[3, 0:2, 0:Y]),
        send(2, 1, 0, soot_hbm.at[X - 2:X], ext.at[4, 0:2, 0:Y]),
        send(3, -1, 0, wind_hbm.at[:, 0:2], ext.at[0:3, X + 2:X + 4, 0:Y]),
        send(4, -1, 0, heat_hbm.at[0:2], ext.at[3, X + 2:X + 4, 0:Y]),
        send(5, -1, 0, soot_hbm.at[0:2], ext.at[4, X + 2:X + 4, 0:Y]),
    ]
    start(fields)

    for c in loads[:3]:
        c.wait()

    def sums(x, _):
        n = count[x]
        terms = [jnp.where(n > k, mass[k, x], 0.0) for k in range(slots)]
        while len(terms) > 1:
            terms = [terms[i] + terms[i + 1] for i in range(0, len(terms) - 1, 2)] + (
                [terms[-1]] if len(terms) % 2 else [])
        zone = label[x]
        onset_here = jnp.full((Y, Z), 1 << 20, jnp.int32)
        for z in range(onset.shape[0]):
            onset_here = jnp.where(zone == z + 1, onset[z], onset_here)
        ext[LOAD, x + 2, 0:Y] = terms[0]
        ext[TALLY, x + 2, 0:Y] = n.astype(jnp.float32)
        ext[SPRAY, x + 2, 0:Y] = jnp.where(onset_here <= 0, inject_rate, 0.0)
        spray_next[x] = jnp.where(onset_here <= 1, inject_rate, 0.0)
        return 0

    lax.fori_loop(0, X, sums, 0)
    drops = [
        send(6, 1, 0, ext.at[LOAD:ALL, X:X + 2, 0:Y], ext.at[LOAD:ALL, 0:2, 0:Y]),
        send(7, -1, 0, ext.at[SPRAY, 2:4, 0:Y], ext.at[SPRAY, X + 2:X + 4, 0:Y]),
    ]
    start(drops)
    for c in loads[3:]:
        c.wait()

    row = lax.broadcasted_iota(jnp.int32, (8, Z), 0)

    def packing(x, _):
        for g in range(2):
            low = high = None
            for j in range(4):
                f = 4 * g + j
                tile_low = ext[f, x + 2, 0:8]
                tile_high = ext[f, x + 2, Y - 8:Y]
                if j == 0:
                    low, high = tile_low, tile_high
                else:
                    here = jnp.logical_and(row >= 2 * j, row < 2 * j + 2)
                    low = jnp.where(here, pltpu.roll(tile_low, 2 * j, 0), low)
                    place = (2 * j + 6) % 8
                    there = jnp.logical_and(row >= place, row < place + 2)
                    high = jnp.where(there, pltpu.roll(tile_high, 2 * j, 0), high)
            pack_low[x, g] = low
            pack_high[x, g] = high
        return 0

    lax.fori_loop(0, X, packing, 0)
    across = [
        send(8, 0, -1, pack_low, from_high.at[1:X + 1]),
        send(9, 0, 1, pack_high, from_low.at[1:X + 1]),
        send(10, -1, -1, pack_low.at[0], from_high.at[X + 1]),
        send(11, 1, -1, pack_low.at[X - 1], from_high.at[0]),
        send(12, -1, 1, pack_high.at[0], from_low.at[X + 1]),
        send(13, 1, 1, pack_high.at[X - 1], from_low.at[0]),
    ]
    start(across)
    masses = [send(14, 1, 0, mass_hbm.at[:, X - 2:X], mass_in)]
    start(masses)

    @pl.when(jnp.logical_not(has[-1]))
    def _():
        ext[:, 0:2] = jnp.zeros((ALL, 2) + ext.shape[2:], jnp.float32)
        from_low[0] = jnp.zeros(from_low.shape[1:], jnp.float32)
        from_high[0] = jnp.zeros(from_low.shape[1:], jnp.float32)
        mass_in[...] = jnp.zeros(mass_in.shape, jnp.float32)

    @pl.when(jnp.logical_not(has[1]))
    def _():
        ext[:, X + 2:X + 4] = jnp.zeros((ALL, 2) + ext.shape[2:], jnp.float32)
        from_low[X + 1] = jnp.zeros(from_low.shape[1:], jnp.float32)
        from_high[X + 1] = jnp.zeros(from_low.shape[1:], jnp.float32)

    @pl.when(jnp.logical_not(has_sec[-1]))
    def _():
        from_low[...] = jnp.zeros(from_low.shape, jnp.float32)

    @pl.when(jnp.logical_not(has_sec[1]))
    def _():
        from_high[...] = jnp.zeros(from_high.shape, jnp.float32)

    wait_recv(fields + drops + across)

    def unpacking(p, _):
        for g in range(2):
            high, low = from_high[p], from_low[p]
            for j in range(4):
                here = jnp.logical_and(row >= 2 * j, row < 2 * j + 2)
                tile = jnp.where(here, high[g], low[g])
                if j:
                    tile = pltpu.roll(tile, 8 - 2 * j, 0)
                ext[4 * g + j, p + 1, Y:Y + 8] = tile
        return 0

    lax.fori_loop(0, X + 2, unpacking, 0)

    lane = lax.broadcasted_iota(jnp.int32, (Y + 8, Z), 1)

    def substep_first(p, carry):
        th_behind, th = carry
        th_ahead = jnp.tanh(ext[3, p + 1])
        q = [ext[f, p] for f in range(FIELDS)]
        behind = [ext[f, p - 1] for f in range(FIELDS)]
        ahead = [ext[f, p + 1] for f in range(FIELDS)]
        fresh = transported(q, behind, ahead, th, th_behind, th_ahead, lane, Y + 8)
        sprayed = ext[LOAD, p - 1] + ext[SPRAY, p] * ext[TALLY, p - 1]
        fresh[3], fresh[4], kept = droplet(fresh[3], fresh[4], sprayed)
        for f in range(FIELDS):
            first[f, p - 1] = fresh[f]
        first[LOAD, p - 1] = kept * sprayed
        kept_first[p - 1] = kept[:Y]
        return th, th_ahead

    lax.fori_loop(1, X + 3, substep_first, (jnp.tanh(ext[3, 0]), jnp.tanh(ext[3, 1])))

    @pl.when(jnp.logical_not(has[-1]))
    def _():
        first[:, 0] = jnp.zeros((first.shape[0],) + first.shape[2:], jnp.float32)

    @pl.when(jnp.logical_not(has[1]))
    def _():
        first[:, X + 1] = jnp.zeros((first.shape[0],) + first.shape[2:], jnp.float32)

    @pl.when(jnp.logical_not(has_sec[-1]))
    def _():
        first[:, :, Y + 7:Y + 8] = jnp.zeros(first.shape[:2] + (1, Z), jnp.float32)

    @pl.when(jnp.logical_not(has_sec[1]))
    def _():
        first[:, :, Y:Y + 1] = jnp.zeros(first.shape[:2] + (1, Z), jnp.float32)

    def substep_second(p, carry):
        th_behind, th = carry
        x = p - 1
        th_ahead = jnp.tanh(first[3, p + 1])
        q = [first[f, p] for f in range(FIELDS)]
        behind = [first[f, p - 1] for f in range(FIELDS)]
        ahead = [first[f, p + 1] for f in range(FIELDS)]
        fresh = transported(q, behind, ahead, th, th_behind, th_ahead, lane, Y)
        tally = ext[TALLY, x, 0:Y]
        spray = spray_next[x]
        sprayed = first[LOAD, p - 1, 0:Y] + spray * tally
        fresh[3], fresh[4], kept = droplet(fresh[3], fresh[4], sprayed)
        for f in range(FIELDS):
            state[f, x] = fresh[f]
        before = kept_first[p - 1]
        coef[0, x] = before * kept
        coef[1, x] = (ext[SPRAY, x + 1, 0:Y] * before + spray) * kept
        coef[2, x] = tally
        return th, th_ahead

    lax.fori_loop(1, X + 1, substep_second, (jnp.tanh(first[3, 0]), jnp.tanh(first[3, 1])))

    wait_recv(masses)
    for a, b, copy in fields + drops + across + masses:
        @pl.when(exists(a, b))
        def _(copy=copy):
            copy.wait_send()


def droplet_kernel(
    chunk, mass_hbm, state, coef, mass_in,
    wind_out, heat_out, soot_out, mass_out, count_out,
    mass, fresh, tally, in_sem, out_sem, state_sem,
):
    slots, X = mass_hbm.shape[:2]
    parts = slots // chunk
    loads = [
        pltpu.make_async_copy(
            mass_hbm.at[pl.ds(i * chunk, chunk), 0:X - 2], mass.at[pl.ds(i * chunk, chunk)],
            in_sem.at[i],
        )
        for i in range(parts)
    ]
    for c in loads:
        c.start()
    moves = [
        pltpu.make_async_copy(state.at[0:3], wind_out, state_sem.at[0]),
        pltpu.make_async_copy(state.at[3], heat_out, state_sem.at[1]),
        pltpu.make_async_copy(state.at[4], soot_out, state_sem.at[2]),
        pltpu.make_async_copy(tally, count_out, state_sem.at[3]),
    ]
    for c in moves[:3]:
        c.start()
    tally[...] = coef[2].astype(jnp.int32)
    moves[3].start()
    stores = []
    for i in range(parts):
        if i == 0:
            def edge(x, _):
                keep, add, n = coef[0, x], coef[1, x], coef[2, x]
                for k in range(slots):
                    m = mass_in[k, x]
                    fresh[k, x] = jnp.where(n > k, keep * m + add, m)
                return 0

            lax.fori_loop(0, 2, edge, 0)
        loads[i].wait()

        def inner(x, _, i=i):
            keep, add, n = coef[0, x], coef[1, x], coef[2, x]
            for k in range(i * chunk, (i + 1) * chunk):
                m = mass[k, x - 2]
                fresh[k, x] = jnp.where(n > k, keep * m + add, m)
            return 0

        lax.fori_loop(2, X, inner, 0)
        span = pl.ds(i * chunk, chunk)
        stores.append(pltpu.make_async_copy(fresh.at[span], mass_out.at[span], out_sem.at[i]))
        stores[-1].start()
    for c in moves + stores:
        c.wait()


def local(tun_size, sec_size, wind, heat, soot, mass, count, label, onset):
    slots, X, Y, Z = mass.shape
    f32 = jnp.float32
    any_spec = pl.BlockSpec(memory_space=pl.ANY)
    vmem_spec = pl.BlockSpec(memory_space=pltpu.VMEM)
    state, coef, mass_in = pl.pallas_call(
        functools.partial(exchange_kernel, tun_size, sec_size),
        out_shape=(
            jax.ShapeDtypeStruct((FIELDS, X, Y, Z), f32),
            jax.ShapeDtypeStruct((3, X, Y, Z), f32),
            jax.ShapeDtypeStruct((slots, 2, Y, Z), f32),
        ),
        in_specs=[any_spec] * 6 + [pl.BlockSpec(memory_space=pltpu.SMEM)],
        out_specs=(vmem_spec,) * 3,
        scratch_shapes=[
            pltpu.VMEM((ALL, X + 4, Y + 8, Z), f32),
            pltpu.VMEM((FIELDS + 1, X + 2, Y + 8, Z), f32),
            pltpu.VMEM((X + 2, Y, Z), f32),
            pltpu.VMEM((X, Y, Z), f32),
            pltpu.VMEM((slots, X, Y, Z), f32),
            pltpu.VMEM((X, Y, Z), jnp.int32),
            pltpu.VMEM((X, Y, Z), jnp.int32),
            pltpu.VMEM((X, 2, 8, Z), f32),
            pltpu.VMEM((X, 2, 8, Z), f32),
            pltpu.VMEM((X + 2, 2, 8, Z), f32),
            pltpu.VMEM((X + 2, 2, 8, Z), f32),
            pltpu.SemaphoreType.DMA((6,)),
            pltpu.SemaphoreType.DMA((15,)),
            pltpu.SemaphoreType.DMA((15,)),
        ],
        compiler_params=pltpu.CompilerParams(
            collective_id=0, has_side_effects=True, vmem_limit_bytes=24 << 20
        ),
        name="fields",
    )(wind, heat, soot, mass, count, label, onset)
    parts = 4
    return pl.pallas_call(
        functools.partial(droplet_kernel, slots // parts),
        out_shape=(
            jax.ShapeDtypeStruct((3, X, Y, Z), f32),
            jax.ShapeDtypeStruct((X, Y, Z), f32),
            jax.ShapeDtypeStruct((X, Y, Z), f32),
            jax.ShapeDtypeStruct((slots, X, Y, Z), f32),
            jax.ShapeDtypeStruct((X, Y, Z), jnp.int32),
        ),
        in_specs=[any_spec, any_spec, vmem_spec, vmem_spec],
        out_specs=(any_spec,) * 5,
        scratch_shapes=[
            pltpu.VMEM((slots, X - 2, Y, Z), f32),
            pltpu.VMEM((slots, X, Y, Z), f32),
            pltpu.VMEM((X, Y, Z), jnp.int32),
            pltpu.SemaphoreType.DMA((parts,)),
            pltpu.SemaphoreType.DMA((parts,)),
            pltpu.SemaphoreType.DMA((4,)),
        ],
        compiler_params=pltpu.CompilerParams(vmem_limit_bytes=24 << 20),
        name="droplets",
    )(mass, state, coef, mass_in)


def solution(mesh):
    return jax.shard_map(
        functools.partial(local, mesh.shape["tun"], mesh.shape["sec"]),
        mesh=mesh,
        in_specs=(
            P(None, "tun", "sec", None),
            P("tun", "sec", None),
            P("tun", "sec", None),
            P(None, "tun", "sec", None),
            P("tun", "sec", None),
            P("tun", "sec", None),
            P(),
        ),
        out_specs=(
            P(None, "tun", "sec", None),
            P("tun", "sec", None),
            P("tun", "sec", None),
            P(None, "tun", "sec", None),
            P("tun", "sec", None),
        ),
        check_vma=False,
    )
```

```python
import functools

import jax
import jax.numpy as jnp
from jax import lax
from jax.experimental import pallas as pl
from jax.experimental.pallas import tpu as pltpu
from jax.sharding import PartitionSpec as P

visc_base = 0.2
time_step = 0.1
buoyancy = 0.5
drag_rate = 0.3
vent_speed = 1.0
inject_rate = 0.5
evap_rate = 0.4
latent_heat = 0.5
scavenge = 0.3

MESH = pl.DeviceIdType.MESH
FIELDS = 5
LOAD, TALLY, SPRAY = 5, 6, 7
ALL = 8


def shifted(c, lane):
    rows, depth = c.shape
    below = pltpu.roll(c, 1, 0)
    above = pltpu.roll(c, rows - 1, 0)
    down = jnp.where(lane == 0, 0.0, pltpu.roll(c, 1, 1))
    up = jnp.where(lane == depth - 1, 0.0, pltpu.roll(c, depth - 1, 1))
    return below, above, down, up


def transported(q, behind, ahead, th, th_behind, th_ahead, lane, keep):
    cut = lambda a: a[:keep]
    around_th = [cut(a) for a in shifted(th, lane)]
    th0 = cut(th)
    half = 0.5 * time_step
    base = 2.0 * visc_base * half
    slope = 0.5 * visc_base * half
    mine = base + slope * th0
    wind = [half * cut(q[d]) for d in range(3)]
    a = [mine + slope * t for t in [cut(th_behind), cut(th_ahead)] + around_th]
    weights = [
        a[0] + wind[0], a[1] - wind[0],
        a[2] + wind[1], a[3] - wind[1],
        a[4] + wind[2], a[5] - wind[2],
    ]
    own = 1.0 - ((a[0] + a[1]) + (a[2] + a[3]) + (a[4] + a[5]))
    fresh = []
    for f in range(FIELDS):
        near = [cut(behind[f]), cut(ahead[f])] + [cut(s) for s in shifted(q[f], lane)]
        terms = [w * n for w, n in zip(weights, near)]
        fresh.append(
            (own * cut(q[f]) + terms[0])
            + (terms[1] + terms[2])
            + (terms[3] + terms[4])
            + terms[5]
        )
    fresh[0] = fresh[0] + time_step * drag_rate * (vent_speed - cut(q[0]))
    fresh[2] = fresh[2] + time_step * buoyancy * cut(q[3])
    return fresh


def droplet(heat, soot, sprayed):
    kept = (1.0 - 0.5 * evap_rate) - 0.5 * evap_rate * jnp.tanh(0.5 * heat)
    heat = heat - latent_heat * (1.0 - kept) * sprayed
    soot = soot / (1.0 + scavenge * sprayed)
    return heat, soot, kept


def exchange_kernel(
    tun_size, sec_size,
    wind_hbm, heat_hbm, soot_hbm, mass_hbm, count_hbm, label_hbm, onset_hbm,
    state, coef, mass_in,
    ext, first, kept_first, spray_next, mass, count, label, onset,
    pack_low, pack_high, from_low, from_high,
    local_sem, send_sem, recv_sem,
):
    X, Y, Z = heat_hbm.shape
    slots = mass_hbm.shape[0]
    t, s = lax.axis_index("tun"), lax.axis_index("sec")
    has = {-1: t > 0, 1: t < tun_size - 1}
    has_sec = {-1: s > 0, 1: s < sec_size - 1}

    def exists(dt, ds):
        if dt and ds:
            return jnp.logical_and(has[dt], has_sec[ds])
        return has[dt] if dt else has_sec[ds]

    around = [(a, b) for a in (-1, 0, 1) for b in (-1, 0, 1) if a or b]

    barrier = pltpu.get_barrier_semaphore()
    for a, b in around:
        @pl.when(exists(a, b))
        def _(a=a, b=b):
            pl.semaphore_signal(
                barrier, inc=1, device_id={"tun": t + a, "sec": s + b}, device_id_type=MESH
            )

    def load(i, src, dst):
        return pltpu.make_async_copy(src, dst, local_sem.at[i])

    loads = [
        load(0, wind_hbm, ext.at[0:3, 2:X + 2, 0:Y]),
        load(1, heat_hbm, ext.at[3, 2:X + 2, 0:Y]),
        load(2, soot_hbm, ext.at[4, 2:X + 2, 0:Y]),
        load(3, count_hbm, count),
        load(4, mass_hbm, mass),
        load(5, label_hbm, label),
        load(6, onset_hbm, onset),
    ]
    for c in loads:
        c.start()

    row = lax.broadcasted_iota(jnp.int32, (8, Z), 0)

    def pack(g):
        def one(x, _):
            low = high = None
            for j in range(4):
                f = 4 * g + j
                tile_low = ext[f, x + 2, 0:8]
                tile_high = ext[f, x + 2, Y - 8:Y]
                if j == 0:
                    low, high = tile_low, tile_high
                else:
                    here = jnp.logical_and(row >= 2 * j, row < 2 * j + 2)
                    low = jnp.where(here, pltpu.roll(tile_low, 2 * j, 0), low)
                    place = (2 * j + 6) % 8
                    there = jnp.logical_and(row >= place, row < place + 2)
                    high = jnp.where(there, pltpu.roll(tile_high, 2 * j, 0), high)
            pack_low[g, x] = low
            pack_high[g, x] = high
            return 0

        lax.fori_loop(0, X, one, 0, unroll=2)

    for c in loads[:3]:
        c.wait()
    pack(0)

    wide = has[-1].astype(jnp.int32) + has[1].astype(jnp.int32)
    deep = has_sec[-1].astype(jnp.int32) + has_sec[1].astype(jnp.int32)
    pl.semaphore_wait(barrier, (1 + wide) * (1 + deep) - 1)

    def send(i, a, b, src, dst):
        return (a, b, pltpu.make_async_remote_copy(
            src_ref=src, dst_ref=dst, send_sem=send_sem.at[i], recv_sem=recv_sem.at[i],
            device_id={"tun": t + a, "sec": s + b}, device_id_type=MESH,
        ))

    def start(group):
        for a, b, copy in group:
            @pl.when(exists(a, b))
            def _(copy=copy):
                copy.start()

    def wait_recv(group):
        for a, b, copy in group:
            @pl.when(exists(-a, -b))
            def _(copy=copy):
                copy.wait_recv()

    fields = [
        send(0, 1, 0, wind_hbm.at[:, X - 2:X], ext.at[0:3, 0:2, 0:Y]),
        send(1, 1, 0, heat_hbm.at[X - 2:X], ext.at[3, 0:2, 0:Y]),
        send(2, 1, 0, soot_hbm.at[X - 2:X], ext.at[4, 0:2, 0:Y]),
        send(3, -1, 0, wind_hbm.at[:, 0:2], ext.at[0:3, X + 2:X + 4, 0:Y]),
        send(4, -1, 0, heat_hbm.at[0:2], ext.at[3, X + 2:X + 4, 0:Y]),
        send(5, -1, 0, soot_hbm.at[0:2], ext.at[4, X + 2:X + 4, 0:Y]),
    ]
    rows_first = [
        send(8, 0, -1, pack_low.at[0], from_high.at[0, 1:X + 1]),
        send(9, 0, 1, pack_high.at[0], from_low.at[0, 1:X + 1]),
    ]
    start(rows_first)
    start(fields)

    for c in loads[3:]:
        c.wait()

    def sums(x, _):
        n = count[x]
        terms = [jnp.where(n > k, mass[k, x], 0.0) for k in range(slots)]
        while len(terms) > 1:
            terms = [terms[i] + terms[i + 1] for i in range(0, len(terms) - 1, 2)] + (
                [terms[-1]] if len(terms) % 2 else [])
        zone = label[x]
        onset_here = jnp.full((Y, Z), 1 << 20, jnp.int32)
        for z in range(onset.shape[0]):
            onset_here = jnp.where(zone == z + 1, onset[z], onset_here)
        ext[LOAD, x + 2, 0:Y] = terms[0]
        ext[TALLY, x + 2, 0:Y] = n.astype(jnp.float32)
        ext[SPRAY, x + 2, 0:Y] = jnp.where(onset_here <= 0, inject_rate, 0.0)
        spray_next[x] = jnp.where(onset_here <= 1, inject_rate, 0.0)
        return 0

    lax.fori_loop(0, X, sums, 0, unroll=2)
    drops = [
        send(6, 1, 0, ext.at[LOAD:ALL, X:X + 2, 0:Y], ext.at[LOAD:ALL, 0:2, 0:Y]),
        send(7, -1, 0, ext.at[SPRAY, 2:4, 0:Y], ext.at[SPRAY, X + 2:X + 4, 0:Y]),
    ]
    start(drops)

    pack(1)
    across = [
        send(10, 0, -1, pack_low.at[1], from_high.at[1, 1:X + 1]),
        send(11, 0, 1, pack_high.at[1], from_low.at[1, 1:X + 1]),
        send(12, -1, -1, pack_low.at[:, 0], from_high.at[:, X + 1]),
        send(13, 1, -1, pack_low.at[:, X - 1], from_high.at[:, 0]),
        send(14, -1, 1, pack_high.at[:, 0], from_low.at[:, X + 1]),
        send(15, 1, 1, pack_high.at[:, X - 1], from_low.at[:, 0]),
    ]
    start(across)
    masses = [send(16, 1, 0, mass_hbm.at[:, X - 2:X], mass_in)]
    start(masses)

    @pl.when(jnp.logical_not(has[-1]))
    def _():
        ext[:, 0:2] = jnp.zeros((ALL, 2) + ext.shape[2:], jnp.float32)
        from_low[:, 0] = jnp.zeros((2, 8, Z), jnp.float32)
        from_high[:, 0] = jnp.zeros((2, 8, Z), jnp.float32)
        mass_in[...] = jnp.zeros(mass_in.shape, jnp.float32)

    @pl.when(jnp.logical_not(has[1]))
    def _():
        ext[:, X + 2:X + 4] = jnp.zeros((ALL, 2) + ext.shape[2:], jnp.float32)
        from_low[:, X + 1] = jnp.zeros((2, 8, Z), jnp.float32)
        from_high[:, X + 1] = jnp.zeros((2, 8, Z), jnp.float32)

    @pl.when(jnp.logical_not(has_sec[-1]))
    def _():
        from_low[...] = jnp.zeros(from_low.shape, jnp.float32)

    @pl.when(jnp.logical_not(has_sec[1]))
    def _():
        from_high[...] = jnp.zeros(from_high.shape, jnp.float32)

    wait_recv(rows_first + fields + drops + across)

    def unpacking(p, _):
        for g in range(2):
            high, low = from_high[g, p], from_low[g, p]
            for j in range(4):
                here = jnp.logical_and(row >= 2 * j, row < 2 * j + 2)
                tile = jnp.where(here, high, low)
                if j:
                    tile = pltpu.roll(tile, 8 - 2 * j, 0)
                ext[4 * g + j, p + 1, Y:Y + 8] = tile
        return 0

    lax.fori_loop(0, X + 2, unpacking, 0, unroll=2)

    lane = lax.broadcasted_iota(jnp.int32, (Y + 8, Z), 1)

    def substep_first(p, carry):
        th_behind, th = carry
        th_ahead = jnp.tanh(ext[3, p + 1])
        q = [ext[f, p] for f in range(FIELDS)]
        behind = [ext[f, p - 1] for f in range(FIELDS)]
        ahead = [ext[f, p + 1] for f in range(FIELDS)]
        fresh = transported(q, behind, ahead, th, th_behind, th_ahead, lane, Y + 8)
        sprayed = ext[LOAD, p - 1] + ext[SPRAY, p] * ext[TALLY, p - 1]
        fresh[3], fresh[4], kept = droplet(fresh[3], fresh[4], sprayed)
        for f in range(FIELDS):
            first[f, p - 1] = fresh[f]
        first[LOAD, p - 1] = kept * sprayed
        kept_first[p - 1] = kept[:Y]
        return th, th_ahead

    lax.fori_loop(1, X + 3, substep_first, (jnp.tanh(ext[3, 0]), jnp.tanh(ext[3, 1])))

    @pl.when(jnp.logical_not(has[-1]))
    def _():
        first[:, 0] = jnp.zeros((first.shape[0],) + first.shape[2:], jnp.float32)

    @pl.when(jnp.logical_not(has[1]))
    def _():
        first[:, X + 1] = jnp.zeros((first.shape[0],) + first.shape[2:], jnp.float32)

    @pl.when(jnp.logical_not(has_sec[-1]))
    def _():
        first[:, :, Y + 7:Y + 8] = jnp.zeros(first.shape[:2] + (1, Z), jnp.float32)

    @pl.when(jnp.logical_not(has_sec[1]))
    def _():
        first[:, :, Y:Y + 1] = jnp.zeros(first.shape[:2] + (1, Z), jnp.float32)

    def substep_second(p, carry):
        th_behind, th = carry
        x = p - 1
        th_ahead = jnp.tanh(first[3, p + 1])
        q = [first[f, p] for f in range(FIELDS)]
        behind = [first[f, p - 1] for f in range(FIELDS)]
        ahead = [first[f, p + 1] for f in range(FIELDS)]
        fresh = transported(q, behind, ahead, th, th_behind, th_ahead, lane, Y)
        tally = ext[TALLY, x, 0:Y]
        spray = spray_next[x]
        sprayed = first[LOAD, p - 1, 0:Y] + spray * tally
        fresh[3], fresh[4], kept = droplet(fresh[3], fresh[4], sprayed)
        for f in range(FIELDS):
            state[f, x] = fresh[f]
        before = kept_first[p - 1]
        coef[0, x] = before * kept
        coef[1, x] = (ext[SPRAY, x + 1, 0:Y] * before + spray) * kept
        coef[2, x] = tally
        return th, th_ahead

    lax.fori_loop(1, X + 1, substep_second, (jnp.tanh(first[3, 0]), jnp.tanh(first[3, 1])))

    wait_recv(masses)
    for a, b, copy in rows_first + fields + drops + across + masses:
        @pl.when(exists(a, b))
        def _(copy=copy):
            copy.wait_send()


def droplet_kernel(
    chunk, mass, state, coef, mass_in,
    wind_out, heat_out, soot_out, mass_out, count_out,
    fresh, tally, out_sem, state_sem,
):
    slots, X = mass.shape[:2]
    parts = slots // chunk
    moves = [
        pltpu.make_async_copy(state.at[0:3], wind_out, state_sem.at[0]),
        pltpu.make_async_copy(state.at[3], heat_out, state_sem.at[1]),
        pltpu.make_async_copy(state.at[4], soot_out, state_sem.at[2]),
        pltpu.make_async_copy(tally, count_out, state_sem.at[3]),
    ]
    for c in moves[:3]:
        c.start()
    tally[...] = coef[2].astype(jnp.int32)
    moves[3].start()
    stores = []
    for i in range(parts):
        if i == 0:
            def edge(x, _):
                keep, add, n = coef[0, x], coef[1, x], coef[2, x]
                for k in range(slots):
                    m = mass_in[k, x]
                    fresh[k, x] = jnp.where(n > k, keep * m + add, m)
                return 0

            lax.fori_loop(0, 2, edge, 0)
        def inner(x, _, i=i):
            keep, add, n = coef[0, x], coef[1, x], coef[2, x]
            for k in range(i * chunk, (i + 1) * chunk):
                m = mass[k, x - 2]
                fresh[k, x] = jnp.where(n > k, keep * m + add, m)
            return 0

        lax.fori_loop(2, X, inner, 0)
        span = pl.ds(i * chunk, chunk)
        stores.append(pltpu.make_async_copy(fresh.at[span], mass_out.at[span], out_sem.at[i]))
        stores[-1].start()
    for c in moves + stores:
        c.wait()


def local(tun_size, sec_size, wind, heat, soot, mass, count, label, onset):
    slots, X, Y, Z = mass.shape
    f32 = jnp.float32
    any_spec = pl.BlockSpec(memory_space=pl.ANY)
    vmem_spec = pl.BlockSpec(memory_space=pltpu.VMEM)
    state, coef, mass_in = pl.pallas_call(
        functools.partial(exchange_kernel, tun_size, sec_size),
        out_shape=(
            jax.ShapeDtypeStruct((FIELDS, X, Y, Z), f32),
            jax.ShapeDtypeStruct((3, X, Y, Z), f32),
            jax.ShapeDtypeStruct((slots, 2, Y, Z), f32),
        ),
        in_specs=[pl.BlockSpec(memory_space=pltpu.HBM)] * 7,
        out_specs=(vmem_spec,) * 3,
        scratch_shapes=[
            pltpu.VMEM((ALL, X + 4, Y + 8, Z), f32),
            pltpu.VMEM((FIELDS + 1, X + 2, Y + 8, Z), f32),
            pltpu.VMEM((X + 2, Y, Z), f32),
            pltpu.VMEM((X, Y, Z), f32),
            pltpu.VMEM((slots, X, Y, Z), f32),
            pltpu.VMEM((X, Y, Z), jnp.int32),
            pltpu.VMEM((X, Y, Z), jnp.int32),
            pltpu.SMEM(onset.shape, jnp.int32),
            pltpu.VMEM((2, X, 8, Z), f32),
            pltpu.VMEM((2, X, 8, Z), f32),
            pltpu.VMEM((2, X + 2, 8, Z), f32),
            pltpu.VMEM((2, X + 2, 8, Z), f32),
            pltpu.SemaphoreType.DMA((7,)),
            pltpu.SemaphoreType.DMA((17,)),
            pltpu.SemaphoreType.DMA((17,)),
        ],
        compiler_params=pltpu.CompilerParams(
            collective_id=0, has_side_effects=True, vmem_limit_bytes=24 << 20
        ),
        name="fields",
    )(*[
        pltpu.with_memory_space_constraint(a, pltpu.HBM)
        for a in (wind, heat, soot, mass, count, label, onset)
    ])
    parts = 4
    return pl.pallas_call(
        functools.partial(droplet_kernel, slots // parts),
        out_shape=(
            jax.ShapeDtypeStruct((3, X, Y, Z), f32),
            jax.ShapeDtypeStruct((X, Y, Z), f32),
            jax.ShapeDtypeStruct((X, Y, Z), f32),
            jax.ShapeDtypeStruct((slots, X, Y, Z), f32),
            jax.ShapeDtypeStruct((X, Y, Z), jnp.int32),
        ),
        in_specs=[vmem_spec, any_spec, vmem_spec, vmem_spec],
        out_specs=(any_spec,) * 5,
        scratch_shapes=[
            pltpu.VMEM((slots, X, Y, Z), f32),
            pltpu.VMEM((X, Y, Z), jnp.int32),
            pltpu.SemaphoreType.DMA((parts,)),
            pltpu.SemaphoreType.DMA((4,)),
        ],
        compiler_params=pltpu.CompilerParams(vmem_limit_bytes=24 << 20),
        name="droplets",
    )(mass, state, coef, mass_in)


def solution(mesh):
    return jax.shard_map(
        functools.partial(local, mesh.shape["tun"], mesh.shape["sec"]),
        mesh=mesh,
        in_specs=(
            P(None, "tun", "sec", None),
            P("tun", "sec", None),
            P("tun", "sec", None),
            P(None, "tun", "sec", None),
            P("tun", "sec", None),
            P("tun", "sec", None),
            P(),
        ),
        out_specs=(
            P(None, "tun", "sec", None),
            P("tun", "sec", None),
            P("tun", "sec", None),
            P(None, "tun", "sec", None),
            P("tun", "sec", None),
        ),
        check_vma=False,
    )
```

```python
import functools

import jax
import jax.numpy as jnp
from jax import lax
from jax.experimental import pallas as pl
from jax.experimental.pallas import tpu as pltpu
from jax.sharding import PartitionSpec as P

visc_base = 0.2
time_step = 0.1
buoyancy = 0.5
drag_rate = 0.3
vent_speed = 1.0
inject_rate = 0.5
evap_rate = 0.4
latent_heat = 0.5
scavenge = 0.3

MESH = pl.DeviceIdType.MESH
FIELDS = 5
LOAD, TALLY, SPRAY = 5, 6, 7
ALL = 8


def shifted(c, lane):
    rows, depth = c.shape
    below = pltpu.roll(c, 1, 0)
    above = pltpu.roll(c, rows - 1, 0)
    down = jnp.where(lane == 0, 0.0, pltpu.roll(c, 1, 1))
    up = jnp.where(lane == depth - 1, 0.0, pltpu.roll(c, depth - 1, 1))
    return below, above, down, up


def transported(q, behind, ahead, th, th_behind, th_ahead, lane, keep):
    cut = lambda a: a[:keep]
    around_th = [cut(a) for a in shifted(th, lane)]
    th0 = cut(th)
    half = 0.5 * time_step
    base = 2.0 * visc_base * half
    slope = 0.5 * visc_base * half
    mine = base + slope * th0
    wind = [half * cut(q[d]) for d in range(3)]
    a = [mine + slope * t for t in [cut(th_behind), cut(th_ahead)] + around_th]
    weights = [
        a[0] + wind[0], a[1] - wind[0],
        a[2] + wind[1], a[3] - wind[1],
        a[4] + wind[2], a[5] - wind[2],
    ]
    own = 1.0 - ((a[0] + a[1]) + (a[2] + a[3]) + (a[4] + a[5]))
    fresh = []
    for f in range(FIELDS):
        near = [cut(behind[f]), cut(ahead[f])] + [cut(s) for s in shifted(q[f], lane)]
        terms = [w * n for w, n in zip(weights, near)]
        fresh.append(
            (own * cut(q[f]) + terms[0])
            + (terms[1] + terms[2])
            + (terms[3] + terms[4])
            + terms[5]
        )
    fresh[0] = fresh[0] + time_step * drag_rate * (vent_speed - cut(q[0]))
    fresh[2] = fresh[2] + time_step * buoyancy * cut(q[3])
    return fresh


def droplet(heat, soot, sprayed):
    kept = (1.0 - 0.5 * evap_rate) - 0.5 * evap_rate * jnp.tanh(0.5 * heat)
    heat = heat - latent_heat * (1.0 - kept) * sprayed
    soot = soot / (1.0 + scavenge * sprayed)
    return heat, soot, kept


def exchange_kernel(
    tun_size, sec_size,
    wind_hbm, heat_hbm, soot_hbm, mass_hbm, count_hbm, label_hbm, onset_hbm,
    state, fresh_mass, tally_out,
    ext, first, kept_first, spray_next, mass, count, label, onset, coef, mass_in,
    pack_low, pack_high, from_low, from_high,
    local_sem, send_sem, recv_sem,
):
    X, Y, Z = heat_hbm.shape
    slots = mass_hbm.shape[0]
    t, s = lax.axis_index("tun"), lax.axis_index("sec")
    has = {-1: t > 0, 1: t < tun_size - 1}
    has_sec = {-1: s > 0, 1: s < sec_size - 1}

    def exists(dt, ds):
        if dt and ds:
            return jnp.logical_and(has[dt], has_sec[ds])
        return has[dt] if dt else has_sec[ds]

    around = [(a, b) for a in (-1, 0, 1) for b in (-1, 0, 1) if a or b]

    barrier = pltpu.get_barrier_semaphore()
    for a, b in around:
        @pl.when(exists(a, b))
        def _(a=a, b=b):
            pl.semaphore_signal(
                barrier, inc=1, device_id={"tun": t + a, "sec": s + b}, device_id_type=MESH
            )

    def load(i, src, dst):
        return pltpu.make_async_copy(src, dst, local_sem.at[i])

    loads = [
        load(0, wind_hbm, ext.at[0:3, 2:X + 2, 0:Y]),
        load(1, heat_hbm, ext.at[3, 2:X + 2, 0:Y]),
        load(2, soot_hbm, ext.at[4, 2:X + 2, 0:Y]),
        load(3, count_hbm, count),
        load(4, mass_hbm, mass),
        load(5, label_hbm, label),
        load(6, onset_hbm, onset),
    ]
    for c in loads:
        c.start()

    row = lax.broadcasted_iota(jnp.int32, (8, Z), 0)

    def pack(g):
        def one(x, _):
            low = high = None
            for j in range(4):
                f = 4 * g + j
                tile_low = ext[f, x + 2, 0:8]
                tile_high = ext[f, x + 2, Y - 8:Y]
                if j == 0:
                    low, high = tile_low, tile_high
                else:
                    here = jnp.logical_and(row >= 2 * j, row < 2 * j + 2)
                    low = jnp.where(here, pltpu.roll(tile_low, 2 * j, 0), low)
                    place = (2 * j + 6) % 8
                    there = jnp.logical_and(row >= place, row < place + 2)
                    high = jnp.where(there, pltpu.roll(tile_high, 2 * j, 0), high)
            pack_low[g, x] = low
            pack_high[g, x] = high
            return 0

        lax.fori_loop(0, X, one, 0, unroll=2)

    for c in loads[:3]:
        c.wait()
    pack(0)

    wide = has[-1].astype(jnp.int32) + has[1].astype(jnp.int32)
    deep = has_sec[-1].astype(jnp.int32) + has_sec[1].astype(jnp.int32)
    pl.semaphore_wait(barrier, (1 + wide) * (1 + deep) - 1)

    def send(i, a, b, src, dst):
        return (a, b, pltpu.make_async_remote_copy(
            src_ref=src, dst_ref=dst, send_sem=send_sem.at[i], recv_sem=recv_sem.at[i],
            device_id={"tun": t + a, "sec": s + b}, device_id_type=MESH,
        ))

    def start(group):
        for a, b, copy in group:
            @pl.when(exists(a, b))
            def _(copy=copy):
                copy.start()

    def wait_recv(group):
        for a, b, copy in group:
            @pl.when(exists(-a, -b))
            def _(copy=copy):
                copy.wait_recv()

    fields = [
        send(0, 1, 0, wind_hbm.at[:, X - 2:X], ext.at[0:3, 0:2, 0:Y]),
        send(1, 1, 0, heat_hbm.at[X - 2:X], ext.at[3, 0:2, 0:Y]),
        send(2, 1, 0, soot_hbm.at[X - 2:X], ext.at[4, 0:2, 0:Y]),
        send(3, -1, 0, wind_hbm.at[:, 0:2], ext.at[0:3, X + 2:X + 4, 0:Y]),
        send(4, -1, 0, heat_hbm.at[0:2], ext.at[3, X + 2:X + 4, 0:Y]),
        send(5, -1, 0, soot_hbm.at[0:2], ext.at[4, X + 2:X + 4, 0:Y]),
    ]
    rows_first = [
        send(8, 0, -1, pack_low.at[0], from_high.at[0, 1:X + 1]),
        send(9, 0, 1, pack_high.at[0], from_low.at[0, 1:X + 1]),
    ]
    start(rows_first)
    start(fields)
    masses = [send(16, 1, 0, mass_hbm.at[:, X - 2:X], mass_in)]
    start(masses)

    for c in loads[3:]:
        c.wait()

    def sums(x, _):
        n = count[x]
        terms = [jnp.where(n > k, mass[k, x], 0.0) for k in range(slots)]
        while len(terms) > 1:
            terms = [terms[i] + terms[i + 1] for i in range(0, len(terms) - 1, 2)] + (
                [terms[-1]] if len(terms) % 2 else [])
        zone = label[x]
        onset_here = jnp.full((Y, Z), 1 << 20, jnp.int32)
        for z in range(onset.shape[0]):
            onset_here = jnp.where(zone == z + 1, onset[z], onset_here)
        ext[LOAD, x + 2, 0:Y] = terms[0]
        ext[TALLY, x + 2, 0:Y] = n.astype(jnp.float32)
        ext[SPRAY, x + 2, 0:Y] = jnp.where(onset_here <= 0, inject_rate, 0.0)
        spray_next[x] = jnp.where(onset_here <= 1, inject_rate, 0.0)
        return 0

    lax.fori_loop(0, X, sums, 0, unroll=2)
    drops = [
        send(6, 1, 0, ext.at[LOAD:ALL, X:X + 2, 0:Y], ext.at[LOAD:ALL, 0:2, 0:Y]),
        send(7, -1, 0, ext.at[SPRAY, 2:4, 0:Y], ext.at[SPRAY, X + 2:X + 4, 0:Y]),
    ]
    start(drops)

    pack(1)
    across = [
        send(10, 0, -1, pack_low.at[1], from_high.at[1, 1:X + 1]),
        send(11, 0, 1, pack_high.at[1], from_low.at[1, 1:X + 1]),
        send(12, -1, -1, pack_low.at[:, 0], from_high.at[:, X + 1]),
        send(13, 1, -1, pack_low.at[:, X - 1], from_high.at[:, 0]),
        send(14, -1, 1, pack_high.at[:, 0], from_low.at[:, X + 1]),
        send(15, 1, 1, pack_high.at[:, X - 1], from_low.at[:, 0]),
    ]
    start(across)

    @pl.when(jnp.logical_not(has[-1]))
    def _():
        ext[:, 0:2] = jnp.zeros((ALL, 2) + ext.shape[2:], jnp.float32)
        from_low[:, 0] = jnp.zeros((2, 8, Z), jnp.float32)
        from_high[:, 0] = jnp.zeros((2, 8, Z), jnp.float32)
        mass_in[...] = jnp.zeros(mass_in.shape, jnp.float32)

    @pl.when(jnp.logical_not(has[1]))
    def _():
        ext[:, X + 2:X + 4] = jnp.zeros((ALL, 2) + ext.shape[2:], jnp.float32)
        from_low[:, X + 1] = jnp.zeros((2, 8, Z), jnp.float32)
        from_high[:, X + 1] = jnp.zeros((2, 8, Z), jnp.float32)

    @pl.when(jnp.logical_not(has_sec[-1]))
    def _():
        from_low[...] = jnp.zeros(from_low.shape, jnp.float32)

    @pl.when(jnp.logical_not(has_sec[1]))
    def _():
        from_high[...] = jnp.zeros(from_high.shape, jnp.float32)

    wait_recv(rows_first + fields[3:] + drops[1:] + across[:2] + [across[2], across[4]])

    def unpacking(p, _):
        for g in range(2):
            high, low = from_high[g, p], from_low[g, p]
            for j in range(4):
                here = jnp.logical_and(row >= 2 * j, row < 2 * j + 2)
                tile = jnp.where(here, high, low)
                if j:
                    tile = pltpu.roll(tile, 8 - 2 * j, 0)
                ext[4 * g + j, p + 1, Y:Y + 8] = tile
        return 0

    lax.fori_loop(1, X + 2, unpacking, 0, unroll=3)

    lane = lax.broadcasted_iota(jnp.int32, (Y + 8, Z), 1)

    def substep_first(p, carry):
        th_behind, th = carry
        th_ahead = jnp.tanh(ext[3, p + 1])
        q = [ext[f, p] for f in range(FIELDS)]
        behind = [ext[f, p - 1] for f in range(FIELDS)]
        ahead = [ext[f, p + 1] for f in range(FIELDS)]
        fresh = transported(q, behind, ahead, th, th_behind, th_ahead, lane, Y + 8)
        sprayed = ext[LOAD, p - 1] + ext[SPRAY, p] * ext[TALLY, p - 1]
        fresh[3], fresh[4], kept = droplet(fresh[3], fresh[4], sprayed)
        for f in range(FIELDS):
            first[f, p - 1] = fresh[f]
        first[LOAD, p - 1] = kept * sprayed
        kept_first[p - 1] = kept[:Y]
        return th, th_ahead

    def first_planes(low, high):
        start_th = (jnp.tanh(ext[3, low - 1]), jnp.tanh(ext[3, low]))
        lax.fori_loop(low, high, substep_first, start_th, unroll=2)

        @pl.when(jnp.logical_not(has_sec[-1]))
        def _():
            first[:, low - 1:high - 1, Y + 7:Y + 8] = jnp.zeros(
                (FIELDS + 1, high - low, 1, Z), jnp.float32)

        @pl.when(jnp.logical_not(has_sec[1]))
        def _():
            first[:, low - 1:high - 1, Y:Y + 1] = jnp.zeros(
                (FIELDS + 1, high - low, 1, Z), jnp.float32)

    def substep_second(p, carry):
        th_behind, th = carry
        x = p - 1
        th_ahead = jnp.tanh(first[3, p + 1])
        q = [first[f, p] for f in range(FIELDS)]
        behind = [first[f, p - 1] for f in range(FIELDS)]
        ahead = [first[f, p + 1] for f in range(FIELDS)]
        fresh = transported(q, behind, ahead, th, th_behind, th_ahead, lane, Y)
        tally = ext[TALLY, x, 0:Y]
        spray = spray_next[x]
        sprayed = first[LOAD, p - 1, 0:Y] + spray * tally
        fresh[3], fresh[4], kept = droplet(fresh[3], fresh[4], sprayed)
        for f in range(FIELDS):
            state[f, x] = fresh[f]
        before = kept_first[p - 1]
        keep, add = before * kept, (ext[SPRAY, x + 1, 0:Y] * before + spray) * kept
        n = tally.astype(jnp.int32)
        tally_out[x] = n
        return keep, add, n, th, th_ahead

    def slot_masses(x, keep, add, n, source, plane):
        for k in range(slots):
            m = source[k, plane]
            fresh_mass[k, x] = jnp.where(n > k, keep * m + add, m)

    def upper(p, carry):
        keep, add, n, th, th_ahead = substep_second(p, carry)
        slot_masses(p - 1, keep, add, n, mass, p - 3)
        return th, th_ahead

    def lowest(p, carry):
        keep, add, n, th, th_ahead = substep_second(p, carry)
        coef[0, p - 1], coef[1, p - 1] = keep, add
        return th, th_ahead

    first_planes(3, X + 3)

    @pl.when(jnp.logical_not(has[1]))
    def _():
        first[:, X + 1] = jnp.zeros((FIELDS + 1, Y + 8, Z), jnp.float32)

    lax.fori_loop(3, X + 1, upper, (jnp.tanh(first[3, 2]), jnp.tanh(first[3, 3])), unroll=2)

    wait_recv(fields[:3] + drops[:1] + [across[3], across[5]])
    unpacking(0, 0)
    first_planes(1, 3)

    @pl.when(jnp.logical_not(has[-1]))
    def _():
        first[:, 0] = jnp.zeros((FIELDS + 1, Y + 8, Z), jnp.float32)

    lax.fori_loop(1, 3, lowest, (jnp.tanh(first[3, 0]), jnp.tanh(first[3, 1])), unroll=2)
    wait_recv(masses)
    for x in range(2):
        slot_masses(x, coef[0, x], coef[1, x], tally_out[x], mass_in, x)
    for a, b, copy in rows_first + fields + drops + across + masses:
        @pl.when(exists(a, b))
        def _(copy=copy):
            copy.wait_send()


def output_kernel(state, mass, tally, wind_out, heat_out, soot_out, mass_out, count_out, sem):
    copies = [
        pltpu.make_async_copy(src, dst, sem.at[i])
        for i, (src, dst) in enumerate([
            (mass, mass_out),
            (state.at[0:3], wind_out),
            (state.at[3], heat_out),
            (state.at[4], soot_out),
            (tally, count_out),
        ])
    ]
    for c in copies:
        c.start()
    for c in copies:
        c.wait()


def local(tun_size, sec_size, wind, heat, soot, mass, count, label, onset):
    slots, X, Y, Z = mass.shape
    f32 = jnp.float32
    any_spec = pl.BlockSpec(memory_space=pl.ANY)
    vmem_spec = pl.BlockSpec(memory_space=pltpu.VMEM)
    state, fresh_mass, tally = pl.pallas_call(
        functools.partial(exchange_kernel, tun_size, sec_size),
        out_shape=(
            jax.ShapeDtypeStruct((FIELDS, X, Y, Z), f32),
            jax.ShapeDtypeStruct((slots, X, Y, Z), f32),
            jax.ShapeDtypeStruct((X, Y, Z), jnp.int32),
        ),
        in_specs=[pl.BlockSpec(memory_space=pltpu.HBM)] * 7,
        out_specs=(vmem_spec,) * 3,
        scratch_shapes=[
            pltpu.VMEM((ALL, X + 4, Y + 8, Z), f32),
            pltpu.VMEM((FIELDS + 1, X + 2, Y + 8, Z), f32),
            pltpu.VMEM((X + 2, Y, Z), f32),
            pltpu.VMEM((X, Y, Z), f32),
            pltpu.VMEM((slots, X, Y, Z), f32),
            pltpu.VMEM((X, Y, Z), jnp.int32),
            pltpu.VMEM((X, Y, Z), jnp.int32),
            pltpu.SMEM(onset.shape, jnp.int32),
            pltpu.VMEM((2, 2, Y, Z), f32),
            pltpu.VMEM((slots, 2, Y, Z), f32),
            pltpu.VMEM((2, X, 8, Z), f32),
            pltpu.VMEM((2, X, 8, Z), f32),
            pltpu.VMEM((2, X + 2, 8, Z), f32),
            pltpu.VMEM((2, X + 2, 8, Z), f32),
            pltpu.SemaphoreType.DMA((7,)),
            pltpu.SemaphoreType.DMA((17,)),
            pltpu.SemaphoreType.DMA((17,)),
        ],
        compiler_params=pltpu.CompilerParams(
            collective_id=0, has_side_effects=True, vmem_limit_bytes=24 << 20
        ),
        name="fields",
    )(*[
        pltpu.with_memory_space_constraint(a, pltpu.HBM)
        for a in (wind, heat, soot, mass, count, label, onset)
    ])
    return pl.pallas_call(
        output_kernel,
        out_shape=(
            jax.ShapeDtypeStruct((3, X, Y, Z), f32),
            jax.ShapeDtypeStruct((X, Y, Z), f32),
            jax.ShapeDtypeStruct((X, Y, Z), f32),
            jax.ShapeDtypeStruct((slots, X, Y, Z), f32),
            jax.ShapeDtypeStruct((X, Y, Z), jnp.int32),
        ),
        in_specs=[vmem_spec] * 3,
        out_specs=(any_spec,) * 5,
        scratch_shapes=[pltpu.SemaphoreType.DMA((5,))],
        compiler_params=pltpu.CompilerParams(vmem_limit_bytes=24 << 20),
        name="outputs",
    )(state, fresh_mass, tally)


def solution(mesh):
    return jax.shard_map(
        functools.partial(local, mesh.shape["tun"], mesh.shape["sec"]),
        mesh=mesh,
        in_specs=(
            P(None, "tun", "sec", None),
            P("tun", "sec", None),
            P("tun", "sec", None),
            P(None, "tun", "sec", None),
            P("tun", "sec", None),
            P("tun", "sec", None),
            P(),
        ),
        out_specs=(
            P(None, "tun", "sec", None),
            P("tun", "sec", None),
            P("tun", "sec", None),
            P(None, "tun", "sec", None),
            P("tun", "sec", None),
        ),
        check_vma=False,
    )
```

```python
import functools

import jax
import jax.numpy as jnp
from jax import lax
from jax.experimental import pallas as pl
from jax.experimental.pallas import tpu as pltpu
from jax.sharding import PartitionSpec as P

visc_base = 0.2
time_step = 0.1
buoyancy = 0.5
drag_rate = 0.3
vent_speed = 1.0
inject_rate = 0.5
evap_rate = 0.4
latent_heat = 0.5
scavenge = 0.3

MESH = pl.DeviceIdType.MESH
FIELDS = 5
LOAD, TALLY, SPRAY = 5, 6, 7
ALL = 8


def shifted(c, lane):
    rows, depth = c.shape
    below = pltpu.roll(c, 1, 0)
    above = pltpu.roll(c, rows - 1, 0)
    down = jnp.where(lane == 0, 0.0, pltpu.roll(c, 1, 1))
    up = jnp.where(lane == depth - 1, 0.0, pltpu.roll(c, depth - 1, 1))
    return below, above, down, up


def transported(q, behind, ahead, th, th_behind, th_ahead, lane, keep):
    cut = lambda a: a[:keep]
    around_th = [cut(a) for a in shifted(th, lane)]
    th0 = cut(th)
    half = 0.5 * time_step
    base = 2.0 * visc_base * half
    slope = 0.5 * visc_base * half
    mine = base + slope * th0
    wind = [half * cut(q[d]) for d in range(3)]
    a = [mine + slope * t for t in [cut(th_behind), cut(th_ahead)] + around_th]
    weights = [
        a[0] + wind[0], a[1] - wind[0],
        a[2] + wind[1], a[3] - wind[1],
        a[4] + wind[2], a[5] - wind[2],
    ]
    own = 1.0 - ((a[0] + a[1]) + (a[2] + a[3]) + (a[4] + a[5]))
    fresh = []
    for f in range(FIELDS):
        near = [cut(behind[f]), cut(ahead[f])] + [cut(s) for s in shifted(q[f], lane)]
        terms = [w * n for w, n in zip(weights, near)]
        fresh.append(
            (own * cut(q[f]) + terms[0])
            + (terms[1] + terms[2])
            + (terms[3] + terms[4])
            + terms[5]
        )
    fresh[0] = fresh[0] + time_step * drag_rate * (vent_speed - cut(q[0]))
    fresh[2] = fresh[2] + time_step * buoyancy * cut(q[3])
    return fresh


def droplet(heat, soot, sprayed):
    kept = (1.0 - 0.5 * evap_rate) - 0.5 * evap_rate * jnp.tanh(0.5 * heat)
    heat = heat - latent_heat * (1.0 - kept) * sprayed
    soot = soot / (1.0 + scavenge * sprayed)
    return heat, soot, kept


def exchange_kernel(
    tun_size, sec_size,
    wind_hbm, heat_hbm, soot_hbm, mass_hbm, count_hbm, label_hbm, onset_hbm,
    state, fresh_mass, tally_out,
    ext, first, kept_first, spray_next, mass, count, label, onset, coef, mass_in,
    pack_low, pack_high, from_low, from_high,
    local_sem, send_sem, recv_sem,
):
    X, Y, Z = heat_hbm.shape
    slots = mass_hbm.shape[0]
    t, s = lax.axis_index("tun"), lax.axis_index("sec")
    has = {-1: t > 0, 1: t < tun_size - 1}
    has_sec = {-1: s > 0, 1: s < sec_size - 1}

    def exists(dt, ds):
        if dt and ds:
            return jnp.logical_and(has[dt], has_sec[ds])
        return has[dt] if dt else has_sec[ds]

    around = [(a, b) for a in (-1, 0, 1) for b in (-1, 0, 1) if a or b]

    barrier = pltpu.get_barrier_semaphore()
    for a, b in around:
        @pl.when(exists(a, b))
        def _(a=a, b=b):
            pl.semaphore_signal(
                barrier, inc=1, device_id={"tun": t + a, "sec": s + b}, device_id_type=MESH
            )

    def load(i, src, dst):
        return pltpu.make_async_copy(src, dst, local_sem.at[i])

    loads = [
        load(0, wind_hbm, ext.at[0:3, 2:X + 2, 0:Y]),
        load(1, heat_hbm, ext.at[3, 2:X + 2, 0:Y]),
        load(2, soot_hbm, ext.at[4, 2:X + 2, 0:Y]),
        load(3, count_hbm, count),
        load(4, mass_hbm, mass),
        load(5, label_hbm, label),
        load(6, onset_hbm, onset),
    ]
    for c in loads:
        c.start()

    row = lax.broadcasted_iota(jnp.int32, (8, Z), 0)

    def pack(g):
        def one(x, _):
            low = high = None
            for j in range(4):
                f = 4 * g + j
                tile_low = ext[f, x + 2, 0:8]
                tile_high = ext[f, x + 2, Y - 8:Y]
                if j == 0:
                    low, high = tile_low, tile_high
                else:
                    here = jnp.logical_and(row >= 2 * j, row < 2 * j + 2)
                    low = jnp.where(here, pltpu.roll(tile_low, 2 * j, 0), low)
                    place = (2 * j + 6) % 8
                    there = jnp.logical_and(row >= place, row < place + 2)
                    high = jnp.where(there, pltpu.roll(tile_high, 2 * j, 0), high)
            pack_low[g, x] = low
            pack_high[g, x] = high
            return 0

        lax.fori_loop(0, X, one, 0, unroll=2)

    wide = has[-1].astype(jnp.int32) + has[1].astype(jnp.int32)
    deep = has_sec[-1].astype(jnp.int32) + has_sec[1].astype(jnp.int32)
    pl.semaphore_wait(barrier, (1 + wide) * (1 + deep) - 1)

    def send(i, a, b, src, dst):
        return (a, b, pltpu.make_async_remote_copy(
            src_ref=src, dst_ref=dst, send_sem=send_sem.at[i], recv_sem=recv_sem.at[i],
            device_id={"tun": t + a, "sec": s + b}, device_id_type=MESH,
        ))

    def start(group):
        for a, b, copy in group:
            @pl.when(exists(a, b))
            def _(copy=copy):
                copy.start()

    def wait_recv(group):
        for a, b, copy in group:
            @pl.when(exists(-a, -b))
            def _(copy=copy):
                copy.wait_recv()

    fields = [
        send(0, 1, 0, wind_hbm.at[:, X - 2:X], ext.at[0:3, 0:2, 0:Y]),
        send(1, 1, 0, heat_hbm.at[X - 2:X], ext.at[3, 0:2, 0:Y]),
        send(2, 1, 0, soot_hbm.at[X - 2:X], ext.at[4, 0:2, 0:Y]),
        send(3, -1, 0, wind_hbm.at[:, 0:2], ext.at[0:3, X + 2:X + 4, 0:Y]),
        send(4, -1, 0, heat_hbm.at[0:2], ext.at[3, X + 2:X + 4, 0:Y]),
        send(5, -1, 0, soot_hbm.at[0:2], ext.at[4, X + 2:X + 4, 0:Y]),
    ]
    start(fields)

    for c in loads[:3]:
        c.wait()
    pack(0)
    rows_first = [
        send(8, 0, -1, pack_low.at[0], from_high.at[0, 1:X + 1]),
        send(9, 0, 1, pack_high.at[0], from_low.at[0, 1:X + 1]),
    ]
    start(rows_first)

    for c in loads[3:]:
        c.wait()

    def sums(x, _):
        n = count[x]
        terms = [jnp.where(n > k, mass[k, x], 0.0) for k in range(slots)]
        while len(terms) > 1:
            terms = [terms[i] + terms[i + 1] for i in range(0, len(terms) - 1, 2)] + (
                [terms[-1]] if len(terms) % 2 else [])
        zone = label[x]
        onset_here = jnp.full((Y, Z), 1 << 20, jnp.int32)
        for z in range(onset.shape[0]):
            onset_here = jnp.where(zone == z + 1, onset[z], onset_here)
        ext[LOAD, x + 2, 0:Y] = terms[0]
        ext[TALLY, x + 2, 0:Y] = n.astype(jnp.float32)
        ext[SPRAY, x + 2, 0:Y] = jnp.where(onset_here <= 0, inject_rate, 0.0)
        spray_next[x] = jnp.where(onset_here <= 1, inject_rate, 0.0)
        return 0

    lax.fori_loop(0, X, sums, 0, unroll=2)
    drops = [
        send(6, 1, 0, ext.at[LOAD:SPRAY, X:X + 2, 0:Y], ext.at[LOAD:SPRAY, 0:2, 0:Y]),
        send(7, 1, 0, ext.at[SPRAY, X + 1, 0:Y], ext.at[SPRAY, 1, 0:Y]),
        send(17, -1, 0, ext.at[SPRAY, 2, 0:Y], ext.at[SPRAY, X + 2, 0:Y]),
    ]
    start(drops)
    masses = [send(16, 1, 0, mass_hbm.at[:, X - 2:X], mass_in)]
    start(masses)

    pack(1)
    across = [
        send(10, 0, -1, pack_low.at[1], from_high.at[1, 1:X + 1]),
        send(11, 0, 1, pack_high.at[1], from_low.at[1, 1:X + 1]),
        send(12, -1, -1, pack_low.at[:, 0], from_high.at[:, X + 1]),
        send(13, 1, -1, pack_low.at[:, X - 1], from_high.at[:, 0]),
        send(14, -1, 1, pack_high.at[:, 0], from_low.at[:, X + 1]),
        send(15, 1, 1, pack_high.at[:, X - 1], from_low.at[:, 0]),
    ]
    start(across)

    @pl.when(jnp.logical_not(has[-1]))
    def _():
        ext[:, 0:2] = jnp.zeros((ALL, 2) + ext.shape[2:], jnp.float32)
        from_low[:, 0] = jnp.zeros((2, 8, Z), jnp.float32)
        from_high[:, 0] = jnp.zeros((2, 8, Z), jnp.float32)
        mass_in[...] = jnp.zeros(mass_in.shape, jnp.float32)

    @pl.when(jnp.logical_not(has[1]))
    def _():
        ext[:, X + 2:X + 4] = jnp.zeros((ALL, 2) + ext.shape[2:], jnp.float32)
        from_low[:, X + 1] = jnp.zeros((2, 8, Z), jnp.float32)
        from_high[:, X + 1] = jnp.zeros((2, 8, Z), jnp.float32)

    @pl.when(jnp.logical_not(has_sec[-1]))
    def _():
        from_low[...] = jnp.zeros(from_low.shape, jnp.float32)

    @pl.when(jnp.logical_not(has_sec[1]))
    def _():
        from_high[...] = jnp.zeros(from_high.shape, jnp.float32)

    wait_recv(rows_first + fields[3:] + drops[2:] + across[:2] + [across[2], across[4]])

    def unpacking(p, _):
        for g in range(2):
            high, low = from_high[g, p], from_low[g, p]
            for j in range(4):
                here = jnp.logical_and(row >= 2 * j, row < 2 * j + 2)
                tile = jnp.where(here, high, low)
                if j:
                    tile = pltpu.roll(tile, 8 - 2 * j, 0)
                ext[4 * g + j, p + 1, Y:Y + 8] = tile
        return 0

    lax.fori_loop(1, X + 2, unpacking, 0, unroll=3)

    lane = lax.broadcasted_iota(jnp.int32, (Y + 8, Z), 1)

    def substep_first(p, carry):
        th_behind, th = carry
        th_ahead = jnp.tanh(ext[3, p + 1])
        q = [ext[f, p] for f in range(FIELDS)]
        behind = [ext[f, p - 1] for f in range(FIELDS)]
        ahead = [ext[f, p + 1] for f in range(FIELDS)]
        fresh = transported(q, behind, ahead, th, th_behind, th_ahead, lane, Y + 8)
        sprayed = ext[LOAD, p - 1] + ext[SPRAY, p] * ext[TALLY, p - 1]
        fresh[3], fresh[4], kept = droplet(fresh[3], fresh[4], sprayed)
        for f in range(FIELDS):
            first[f, p - 1] = fresh[f]
        first[LOAD, p - 1] = kept * sprayed
        kept_first[p - 1] = kept[:Y]
        return th, th_ahead

    def first_planes(low, high):
        start_th = (jnp.tanh(ext[3, low - 1]), jnp.tanh(ext[3, low]))
        lax.fori_loop(low, high, substep_first, start_th, unroll=2)

        @pl.when(jnp.logical_not(has_sec[-1]))
        def _():
            first[:, low - 1:high - 1, Y + 7:Y + 8] = jnp.zeros(
                (FIELDS + 1, high - low, 1, Z), jnp.float32)

        @pl.when(jnp.logical_not(has_sec[1]))
        def _():
            first[:, low - 1:high - 1, Y:Y + 1] = jnp.zeros(
                (FIELDS + 1, high - low, 1, Z), jnp.float32)

    def substep_second(p, carry):
        th_behind, th = carry
        x = p - 1
        th_ahead = jnp.tanh(first[3, p + 1])
        q = [first[f, p] for f in range(FIELDS)]
        behind = [first[f, p - 1] for f in range(FIELDS)]
        ahead = [first[f, p + 1] for f in range(FIELDS)]
        fresh = transported(q, behind, ahead, th, th_behind, th_ahead, lane, Y)
        tally = ext[TALLY, x, 0:Y]
        spray = spray_next[x]
        sprayed = first[LOAD, p - 1, 0:Y] + spray * tally
        fresh[3], fresh[4], kept = droplet(fresh[3], fresh[4], sprayed)
        for f in range(FIELDS):
            state[f, x] = fresh[f]
        before = kept_first[p - 1]
        keep, add = before * kept, (ext[SPRAY, x + 1, 0:Y] * before + spray) * kept
        n = tally.astype(jnp.int32)
        tally_out[x] = n
        return keep, add, n, th, th_ahead

    def slot_masses(x, keep, add, n, source, plane):
        for k in range(slots):
            m = source[k, plane]
            fresh_mass[k, x] = jnp.where(n > k, keep * m + add, m)

    def upper(p, carry):
        keep, add, n, th, th_ahead = substep_second(p, carry)
        slot_masses(p - 1, keep, add, n, mass, p - 3)
        return th, th_ahead

    def lowest(p, carry):
        keep, add, n, th, th_ahead = substep_second(p, carry)
        coef[0, p - 1], coef[1, p - 1] = keep, add
        return th, th_ahead

    first_planes(3, X + 3)

    @pl.when(jnp.logical_not(has[1]))
    def _():
        first[:, X + 1] = jnp.zeros((FIELDS + 1, Y + 8, Z), jnp.float32)

    lax.fori_loop(3, X + 1, upper, (jnp.tanh(first[3, 2]), jnp.tanh(first[3, 3])), unroll=2)

    wait_recv(fields[:3] + drops[:2] + [across[3], across[5]])
    unpacking(0, 0)
    first_planes(1, 3)

    @pl.when(jnp.logical_not(has[-1]))
    def _():
        first[:, 0] = jnp.zeros((FIELDS + 1, Y + 8, Z), jnp.float32)

    lax.fori_loop(1, 3, lowest, (jnp.tanh(first[3, 0]), jnp.tanh(first[3, 1])), unroll=2)
    wait_recv(masses)
    for x in range(2):
        slot_masses(x, coef[0, x], coef[1, x], tally_out[x], mass_in, x)
    for a, b, copy in rows_first + fields + drops + across + masses:
        @pl.when(exists(a, b))
        def _(copy=copy):
            copy.wait_send()


def output_kernel(state, mass, tally, wind_out, heat_out, soot_out, mass_out, count_out, sem):
    copies = [
        pltpu.make_async_copy(src, dst, sem.at[i])
        for i, (src, dst) in enumerate([
            (mass, mass_out),
            (state.at[0:3], wind_out),
            (state.at[3], heat_out),
            (state.at[4], soot_out),
            (tally, count_out),
        ])
    ]
    for c in copies:
        c.start()
    for c in copies:
        c.wait()


def local(tun_size, sec_size, wind, heat, soot, mass, count, label, onset):
    slots, X, Y, Z = mass.shape
    f32 = jnp.float32
    any_spec = pl.BlockSpec(memory_space=pl.ANY)
    vmem_spec = pl.BlockSpec(memory_space=pltpu.VMEM)
    state, fresh_mass, tally = pl.pallas_call(
        functools.partial(exchange_kernel, tun_size, sec_size),
        out_shape=(
            jax.ShapeDtypeStruct((FIELDS, X, Y, Z), f32),
            jax.ShapeDtypeStruct((slots, X, Y, Z), f32),
            jax.ShapeDtypeStruct((X, Y, Z), jnp.int32),
        ),
        in_specs=[pl.BlockSpec(memory_space=pltpu.HBM)] * 7,
        out_specs=(vmem_spec,) * 3,
        scratch_shapes=[
            pltpu.VMEM((ALL, X + 4, Y + 8, Z), f32),
            pltpu.VMEM((FIELDS + 1, X + 2, Y + 8, Z), f32),
            pltpu.VMEM((X + 2, Y, Z), f32),
            pltpu.VMEM((X, Y, Z), f32),
            pltpu.VMEM((slots, X, Y, Z), f32),
            pltpu.VMEM((X, Y, Z), jnp.int32),
            pltpu.VMEM((X, Y, Z), jnp.int32),
            pltpu.SMEM(onset.shape, jnp.int32),
            pltpu.VMEM((2, 2, Y, Z), f32),
            pltpu.VMEM((slots, 2, Y, Z), f32),
            pltpu.VMEM((2, X, 8, Z), f32),
            pltpu.VMEM((2, X, 8, Z), f32),
            pltpu.VMEM((2, X + 2, 8, Z), f32),
            pltpu.VMEM((2, X + 2, 8, Z), f32),
            pltpu.SemaphoreType.DMA((7,)),
            pltpu.SemaphoreType.DMA((18,)),
            pltpu.SemaphoreType.DMA((18,)),
        ],
        compiler_params=pltpu.CompilerParams(
            collective_id=0, has_side_effects=True, vmem_limit_bytes=24 << 20
        ),
        name="fields",
    )(*[
        pltpu.with_memory_space_constraint(a, pltpu.HBM)
        for a in (wind, heat, soot, mass, count, label, onset)
    ])
    return pl.pallas_call(
        output_kernel,
        out_shape=(
            jax.ShapeDtypeStruct((3, X, Y, Z), f32),
            jax.ShapeDtypeStruct((X, Y, Z), f32),
            jax.ShapeDtypeStruct((X, Y, Z), f32),
            jax.ShapeDtypeStruct((slots, X, Y, Z), f32),
            jax.ShapeDtypeStruct((X, Y, Z), jnp.int32),
        ),
        in_specs=[vmem_spec] * 3,
        out_specs=(any_spec,) * 5,
        scratch_shapes=[pltpu.SemaphoreType.DMA((5,))],
        compiler_params=pltpu.CompilerParams(vmem_limit_bytes=24 << 20),
        name="outputs",
    )(state, fresh_mass, tally)


def solution(mesh):
    return jax.shard_map(
        functools.partial(local, mesh.shape["tun"], mesh.shape["sec"]),
        mesh=mesh,
        in_specs=(
            P(None, "tun", "sec", None),
            P("tun", "sec", None),
            P("tun", "sec", None),
            P(None, "tun", "sec", None),
            P("tun", "sec", None),
            P("tun", "sec", None),
            P(),
        ),
        out_specs=(
            P(None, "tun", "sec", None),
            P("tun", "sec", None),
            P("tun", "sec", None),
            P(None, "tun", "sec", None),
            P("tun", "sec", None),
        ),
        check_vma=False,
    )
```

```python
import functools

import jax
import jax.numpy as jnp
from jax import lax
from jax.experimental import pallas as pl
from jax.experimental.pallas import tpu as pltpu
from jax.sharding import PartitionSpec as P

visc_base = 0.2
time_step = 0.1
buoyancy = 0.5
drag_rate = 0.3
vent_speed = 1.0
inject_rate = 0.5
evap_rate = 0.4
latent_heat = 0.5
scavenge = 0.3

MESH = pl.DeviceIdType.MESH
FIELDS = 5
LOAD, TALLY, SPRAY = 5, 6, 7
ALL = 8


def shifted(c, lane):
    rows, depth = c.shape
    below = pltpu.roll(c, 1, 0)
    above = pltpu.roll(c, rows - 1, 0)
    down = jnp.where(lane == 0, 0.0, pltpu.roll(c, 1, 1))
    up = jnp.where(lane == depth - 1, 0.0, pltpu.roll(c, depth - 1, 1))
    return below, above, down, up


def transported(q, behind, ahead, th, th_behind, th_ahead, lane, keep):
    cut = lambda a: a[:keep]
    around_th = [cut(a) for a in shifted(th, lane)]
    th0 = cut(th)
    half = 0.5 * time_step
    base = 2.0 * visc_base * half
    slope = 0.5 * visc_base * half
    mine = base + slope * th0
    wind = [half * cut(q[d]) for d in range(3)]
    a = [mine + slope * t for t in [cut(th_behind), cut(th_ahead)] + around_th]
    weights = [
        a[0] + wind[0], a[1] - wind[0],
        a[2] + wind[1], a[3] - wind[1],
        a[4] + wind[2], a[5] - wind[2],
    ]
    own = 1.0 - ((a[0] + a[1]) + (a[2] + a[3]) + (a[4] + a[5]))
    fresh = []
    for f in range(FIELDS):
        near = [cut(behind[f]), cut(ahead[f])] + [cut(s) for s in shifted(q[f], lane)]
        terms = [w * n for w, n in zip(weights, near)]
        fresh.append(
            (own * cut(q[f]) + terms[0])
            + (terms[1] + terms[2])
            + (terms[3] + terms[4])
            + terms[5]
        )
    fresh[0] = fresh[0] + time_step * drag_rate * (vent_speed - cut(q[0]))
    fresh[2] = fresh[2] + time_step * buoyancy * cut(q[3])
    return fresh


def droplet(heat, soot, sprayed):
    kept = (1.0 - 0.5 * evap_rate) - 0.5 * evap_rate * jnp.tanh(0.5 * heat)
    heat = heat - latent_heat * (1.0 - kept) * sprayed
    soot = soot / (1.0 + scavenge * sprayed)
    return heat, soot, kept


def exchange_kernel(
    tun_size, sec_size, parts,
    wind_hbm, heat_hbm, soot_hbm, mass_hbm, count_hbm, label_hbm, onset_hbm,
    state, fresh_mass, tally_out,
    ext, first, kept_first, spray_next, mass, count, label, onset, coef, mass_in,
    pack_low, pack_high, from_low, from_high,
    local_sem, send_sem, recv_sem,
):
    X, Y, Z = heat_hbm.shape
    slots = mass_hbm.shape[0]
    t, s = lax.axis_index("tun"), lax.axis_index("sec")
    has = {-1: t > 0, 1: t < tun_size - 1}
    has_sec = {-1: s > 0, 1: s < sec_size - 1}

    def exists(dt, ds):
        if dt and ds:
            return jnp.logical_and(has[dt], has_sec[ds])
        return has[dt] if dt else has_sec[ds]

    around = [(a, b) for a in (-1, 0, 1) for b in (-1, 0, 1) if a or b]

    barrier = pltpu.get_barrier_semaphore()
    for a, b in around:
        @pl.when(exists(a, b))
        def _(a=a, b=b):
            pl.semaphore_signal(
                barrier, inc=1, device_id={"tun": t + a, "sec": s + b}, device_id_type=MESH
            )

    def load(i, src, dst):
        return pltpu.make_async_copy(src, dst, local_sem.at[i])

    loads = [
        load(0, wind_hbm, ext.at[0:3, 2:X + 2, 0:Y]),
        load(1, heat_hbm, ext.at[3, 2:X + 2, 0:Y]),
        load(2, soot_hbm, ext.at[4, 2:X + 2, 0:Y]),
        load(3, count_hbm, count),
        load(4, mass_hbm, mass),
        load(5, label_hbm, label),
        load(6, onset_hbm, onset),
    ]
    for c in loads:
        c.start()

    row = lax.broadcasted_iota(jnp.int32, (8, Z), 0)

    def pack(g):
        def one(x, _):
            low = high = None
            for j in range(4):
                f = 4 * g + j
                tile_low = ext[f, x + 2, 0:8]
                tile_high = ext[f, x + 2, Y - 8:Y]
                if j == 0:
                    low, high = tile_low, tile_high
                else:
                    here = jnp.logical_and(row >= 2 * j, row < 2 * j + 2)
                    low = jnp.where(here, pltpu.roll(tile_low, 2 * j, 0), low)
                    place = (2 * j + 6) % 8
                    there = jnp.logical_and(row >= place, row < place + 2)
                    high = jnp.where(there, pltpu.roll(tile_high, 2 * j, 0), high)
            pack_low[g, x] = low
            pack_high[g, x] = high
            return 0

        lax.fori_loop(0, X, one, 0, unroll=2)

    wide = has[-1].astype(jnp.int32) + has[1].astype(jnp.int32)
    deep = has_sec[-1].astype(jnp.int32) + has_sec[1].astype(jnp.int32)
    pl.semaphore_wait(barrier, (1 + wide) * (1 + deep) - 1)

    def send(i, a, b, src, dst):
        return (a, b, pltpu.make_async_remote_copy(
            src_ref=src, dst_ref=dst, send_sem=send_sem.at[i], recv_sem=recv_sem.at[i],
            device_id={"tun": t + a, "sec": s + b}, device_id_type=MESH,
        ))

    def start(group):
        for a, b, copy in group:
            @pl.when(exists(a, b))
            def _(copy=copy):
                copy.start()

    def wait_recv(group):
        for a, b, copy in group:
            @pl.when(exists(-a, -b))
            def _(copy=copy):
                copy.wait_recv()

    fields = [
        send(0, 1, 0, wind_hbm.at[:, X - 2:X], ext.at[0:3, 0:2, 0:Y]),
        send(1, 1, 0, heat_hbm.at[X - 2:X], ext.at[3, 0:2, 0:Y]),
        send(2, 1, 0, soot_hbm.at[X - 2:X], ext.at[4, 0:2, 0:Y]),
        send(3, -1, 0, wind_hbm.at[:, 0:2], ext.at[0:3, X + 2:X + 4, 0:Y]),
        send(4, -1, 0, heat_hbm.at[0:2], ext.at[3, X + 2:X + 4, 0:Y]),
        send(5, -1, 0, soot_hbm.at[0:2], ext.at[4, X + 2:X + 4, 0:Y]),
    ]
    start(fields)

    for c in loads[:3]:
        c.wait()
    pack(0)
    rows_first = [
        send(8, 0, -1, pack_low.at[0], from_high.at[0, 1:X + 1]),
        send(9, 0, 1, pack_high.at[0], from_low.at[0, 1:X + 1]),
    ]
    start(rows_first)

    for c in loads[3:]:
        c.wait()

    def sums(x, _):
        n = count[x]
        terms = [jnp.where(n > k, mass[k, x], 0.0) for k in range(slots)]
        while len(terms) > 1:
            terms = [terms[i] + terms[i + 1] for i in range(0, len(terms) - 1, 2)] + (
                [terms[-1]] if len(terms) % 2 else [])
        zone = label[x]
        onset_here = jnp.full((Y, Z), 1 << 20, jnp.int32)
        for z in range(onset.shape[0]):
            onset_here = jnp.where(zone == z + 1, onset[z], onset_here)
        ext[LOAD, x + 2, 0:Y] = terms[0]
        ext[TALLY, x + 2, 0:Y] = n.astype(jnp.float32)
        ext[SPRAY, x + 2, 0:Y] = jnp.where(onset_here <= 0, inject_rate, 0.0)
        spray_next[x] = jnp.where(onset_here <= 1, inject_rate, 0.0)
        return 0

    lax.fori_loop(0, X, sums, 0, unroll=2)
    drops = [
        send(6, 1, 0, ext.at[LOAD:SPRAY, X:X + 2, 0:Y], ext.at[LOAD:SPRAY, 0:2, 0:Y]),
        send(7, 1, 0, ext.at[SPRAY, X + 1, 0:Y], ext.at[SPRAY, 1, 0:Y]),
        send(16, -1, 0, ext.at[SPRAY, 2, 0:Y], ext.at[SPRAY, X + 2, 0:Y]),
    ]
    start(drops)
    group = slots // parts
    masses = [
        send(17 + i, 1, 0, mass.at[i * group:(i + 1) * group, X - 2:X],
             mass_in.at[i * group:(i + 1) * group])
        for i in range(parts)
    ]
    start(masses)

    pack(1)
    across = [
        send(10, 0, -1, pack_low.at[1], from_high.at[1, 1:X + 1]),
        send(11, 0, 1, pack_high.at[1], from_low.at[1, 1:X + 1]),
        send(12, -1, -1, pack_low.at[:, 0], from_high.at[:, X + 1]),
        send(13, 1, -1, pack_low.at[:, X - 1], from_high.at[:, 0]),
        send(14, -1, 1, pack_high.at[:, 0], from_low.at[:, X + 1]),
        send(15, 1, 1, pack_high.at[:, X - 1], from_low.at[:, 0]),
    ]
    start(across)

    @pl.when(jnp.logical_not(has[-1]))
    def _():
        ext[:, 0:2] = jnp.zeros((ALL, 2) + ext.shape[2:], jnp.float32)
        from_low[:, 0] = jnp.zeros((2, 8, Z), jnp.float32)
        from_high[:, 0] = jnp.zeros((2, 8, Z), jnp.float32)
        mass_in[...] = jnp.zeros(mass_in.shape, jnp.float32)

    @pl.when(jnp.logical_not(has[1]))
    def _():
        ext[:, X + 2:X + 4] = jnp.zeros((ALL, 2) + ext.shape[2:], jnp.float32)
        from_low[:, X + 1] = jnp.zeros((2, 8, Z), jnp.float32)
        from_high[:, X + 1] = jnp.zeros((2, 8, Z), jnp.float32)

    @pl.when(jnp.logical_not(has_sec[-1]))
    def _():
        from_low[...] = jnp.zeros(from_low.shape, jnp.float32)

    @pl.when(jnp.logical_not(has_sec[1]))
    def _():
        from_high[...] = jnp.zeros(from_high.shape, jnp.float32)

    wait_recv(rows_first + fields[3:] + drops[2:] + across[:2] + [across[2], across[4]])

    def unpacking(p, _):
        for g in range(2):
            high, low = from_high[g, p], from_low[g, p]
            for j in range(4):
                here = jnp.logical_and(row >= 2 * j, row < 2 * j + 2)
                tile = jnp.where(here, high, low)
                if j:
                    tile = pltpu.roll(tile, 8 - 2 * j, 0)
                ext[4 * g + j, p + 1, Y:Y + 8] = tile
        return 0

    lax.fori_loop(1, X + 2, unpacking, 0, unroll=3)

    lane = lax.broadcasted_iota(jnp.int32, (Y + 8, Z), 1)

    def substep_first(p, carry):
        th_behind, th = carry
        th_ahead = jnp.tanh(ext[3, p + 1])
        q = [ext[f, p] for f in range(FIELDS)]
        behind = [ext[f, p - 1] for f in range(FIELDS)]
        ahead = [ext[f, p + 1] for f in range(FIELDS)]
        fresh = transported(q, behind, ahead, th, th_behind, th_ahead, lane, Y + 8)
        sprayed = ext[LOAD, p - 1] + ext[SPRAY, p] * ext[TALLY, p - 1]
        fresh[3], fresh[4], kept = droplet(fresh[3], fresh[4], sprayed)
        for f in range(FIELDS):
            first[f, p - 1] = fresh[f]
        first[LOAD, p - 1] = kept * sprayed
        kept_first[p - 1] = kept[:Y]
        return th, th_ahead

    def first_planes(low, high):
        start_th = (jnp.tanh(ext[3, low - 1]), jnp.tanh(ext[3, low]))
        lax.fori_loop(low, high, substep_first, start_th, unroll=2)

        @pl.when(jnp.logical_not(has_sec[-1]))
        def _():
            first[:, low - 1:high - 1, Y + 7:Y + 8] = jnp.zeros(
                (FIELDS + 1, high - low, 1, Z), jnp.float32)

        @pl.when(jnp.logical_not(has_sec[1]))
        def _():
            first[:, low - 1:high - 1, Y:Y + 1] = jnp.zeros(
                (FIELDS + 1, high - low, 1, Z), jnp.float32)

    def substep_second(p, carry):
        th_behind, th = carry
        x = p - 1
        th_ahead = jnp.tanh(first[3, p + 1])
        q = [first[f, p] for f in range(FIELDS)]
        behind = [first[f, p - 1] for f in range(FIELDS)]
        ahead = [first[f, p + 1] for f in range(FIELDS)]
        fresh = transported(q, behind, ahead, th, th_behind, th_ahead, lane, Y)
        tally = ext[TALLY, x, 0:Y]
        spray = spray_next[x]
        sprayed = first[LOAD, p - 1, 0:Y] + spray * tally
        fresh[3], fresh[4], kept = droplet(fresh[3], fresh[4], sprayed)
        for f in range(FIELDS):
            state[f, x] = fresh[f]
        before = kept_first[p - 1]
        keep, add = before * kept, (ext[SPRAY, x + 1, 0:Y] * before + spray) * kept
        n = tally.astype(jnp.int32)
        tally_out[x] = n
        return keep, add, n, th, th_ahead

    def slot_masses(x, keep, add, n, source, plane, which=range(slots)):
        for k in which:
            m = source[k, plane]
            fresh_mass[k, x] = jnp.where(n > k, keep * m + add, m)

    def upper(p, carry):
        keep, add, n, th, th_ahead = substep_second(p, carry)
        slot_masses(p - 1, keep, add, n, mass, p - 3)
        return th, th_ahead

    def lowest(p, carry):
        keep, add, n, th, th_ahead = substep_second(p, carry)
        coef[0, p - 1], coef[1, p - 1] = keep, add
        return th, th_ahead

    first_planes(3, X + 3)

    @pl.when(jnp.logical_not(has[1]))
    def _():
        first[:, X + 1] = jnp.zeros((FIELDS + 1, Y + 8, Z), jnp.float32)

    lax.fori_loop(3, X + 1, upper, (jnp.tanh(first[3, 2]), jnp.tanh(first[3, 3])), unroll=2)

    wait_recv(fields[:3] + drops[:2] + [across[3], across[5]])
    unpacking(0, 0)
    first_planes(1, 3)

    @pl.when(jnp.logical_not(has[-1]))
    def _():
        first[:, 0] = jnp.zeros((FIELDS + 1, Y + 8, Z), jnp.float32)

    lax.fori_loop(1, 3, lowest, (jnp.tanh(first[3, 0]), jnp.tanh(first[3, 1])), unroll=2)
    for i in range(parts):
        wait_recv(masses[i:i + 1])
        for x in range(2):
            slot_masses(x, coef[0, x], coef[1, x], tally_out[x], mass_in, x,
                        range(i * group, (i + 1) * group))
    for a, b, copy in rows_first + fields + drops + across + masses:
        @pl.when(exists(a, b))
        def _(copy=copy):
            copy.wait_send()


def output_kernel(state, mass, tally, wind_out, heat_out, soot_out, mass_out, count_out, sem):
    copies = [
        pltpu.make_async_copy(src, dst, sem.at[i])
        for i, (src, dst) in enumerate([
            (mass, mass_out),
            (state.at[0:3], wind_out),
            (state.at[3], heat_out),
            (state.at[4], soot_out),
            (tally, count_out),
        ])
    ]
    for c in copies:
        c.start()
    for c in copies:
        c.wait()


def local(tun_size, sec_size, wind, heat, soot, mass, count, label, onset):
    slots, X, Y, Z = mass.shape
    f32 = jnp.float32
    parts = 4 if slots % 4 == 0 else 1
    any_spec = pl.BlockSpec(memory_space=pl.ANY)
    vmem_spec = pl.BlockSpec(memory_space=pltpu.VMEM)
    state, fresh_mass, tally = pl.pallas_call(
        functools.partial(exchange_kernel, tun_size, sec_size, parts),
        out_shape=(
            jax.ShapeDtypeStruct((FIELDS, X, Y, Z), f32),
            jax.ShapeDtypeStruct((slots, X, Y, Z), f32),
            jax.ShapeDtypeStruct((X, Y, Z), jnp.int32),
        ),
        in_specs=[pl.BlockSpec(memory_space=pltpu.HBM)] * 7,
        out_specs=(vmem_spec,) * 3,
        scratch_shapes=[
            pltpu.VMEM((ALL, X + 4, Y + 8, Z), f32),
            pltpu.VMEM((FIELDS + 1, X + 2, Y + 8, Z), f32),
            pltpu.VMEM((X + 2, Y, Z), f32),
            pltpu.VMEM((X, Y, Z), f32),
            pltpu.VMEM((slots, X, Y, Z), f32),
            pltpu.VMEM((X, Y, Z), jnp.int32),
            pltpu.VMEM((X, Y, Z), jnp.int32),
            pltpu.SMEM(onset.shape, jnp.int32),
            pltpu.VMEM((2, 2, Y, Z), f32),
            pltpu.VMEM((slots, 2, Y, Z), f32),
            pltpu.VMEM((2, X, 8, Z), f32),
            pltpu.VMEM((2, X, 8, Z), f32),
            pltpu.VMEM((2, X + 2, 8, Z), f32),
            pltpu.VMEM((2, X + 2, 8, Z), f32),
            pltpu.SemaphoreType.DMA((7,)),
            pltpu.SemaphoreType.DMA((17 + parts,)),
            pltpu.SemaphoreType.DMA((17 + parts,)),
        ],
        compiler_params=pltpu.CompilerParams(
            collective_id=0, has_side_effects=True, vmem_limit_bytes=24 << 20
        ),
        name="fields",
    )(*[
        pltpu.with_memory_space_constraint(a, pltpu.HBM)
        for a in (wind, heat, soot, mass, count, label, onset)
    ])
    return pl.pallas_call(
        output_kernel,
        out_shape=(
            jax.ShapeDtypeStruct((3, X, Y, Z), f32),
            jax.ShapeDtypeStruct((X, Y, Z), f32),
            jax.ShapeDtypeStruct((X, Y, Z), f32),
            jax.ShapeDtypeStruct((slots, X, Y, Z), f32),
            jax.ShapeDtypeStruct((X, Y, Z), jnp.int32),
        ),
        in_specs=[vmem_spec] * 3,
        out_specs=(any_spec,) * 5,
        scratch_shapes=[pltpu.SemaphoreType.DMA((5,))],
        compiler_params=pltpu.CompilerParams(vmem_limit_bytes=24 << 20),
        name="outputs",
    )(state, fresh_mass, tally)


def solution(mesh):
    return jax.shard_map(
        functools.partial(local, mesh.shape["tun"], mesh.shape["sec"]),
        mesh=mesh,
        in_specs=(
            P(None, "tun", "sec", None),
            P("tun", "sec", None),
            P("tun", "sec", None),
            P(None, "tun", "sec", None),
            P("tun", "sec", None),
            P("tun", "sec", None),
            P(),
        ),
        out_specs=(
            P(None, "tun", "sec", None),
            P("tun", "sec", None),
            P("tun", "sec", None),
            P(None, "tun", "sec", None),
            P("tun", "sec", None),
        ),
        check_vma=False,
    )
```

```python
import functools

import jax
import jax.numpy as jnp
from jax import lax
from jax.experimental import pallas as pl
from jax.experimental.pallas import tpu as pltpu
from jax.sharding import PartitionSpec as P

visc_base = 0.2
time_step = 0.1
buoyancy = 0.5
drag_rate = 0.3
vent_speed = 1.0
inject_rate = 0.5
evap_rate = 0.4
latent_heat = 0.5
scavenge = 0.3

MESH = pl.DeviceIdType.MESH
FIELDS = 5
LOAD, TALLY, SPRAY = 5, 6, 7
ALL = 8


def shifted(c, lane):
    rows, depth = c.shape
    below = pltpu.roll(c, 1, 0)
    above = pltpu.roll(c, rows - 1, 0)
    down = jnp.where(lane == 0, 0.0, pltpu.roll(c, 1, 1))
    up = jnp.where(lane == depth - 1, 0.0, pltpu.roll(c, depth - 1, 1))
    return below, above, down, up


def transported(q, behind, ahead, th, th_behind, th_ahead, lane, keep):
    cut = lambda a: a[:keep]
    around_th = [cut(a) for a in shifted(th, lane)]
    th0 = cut(th)
    half = 0.5 * time_step
    base = 2.0 * visc_base * half
    slope = 0.5 * visc_base * half
    mine = base + slope * th0
    wind = [half * cut(q[d]) for d in range(3)]
    a = [mine + slope * t for t in [cut(th_behind), cut(th_ahead)] + around_th]
    weights = [
        a[0] + wind[0], a[1] - wind[0],
        a[2] + wind[1], a[3] - wind[1],
        a[4] + wind[2], a[5] - wind[2],
    ]
    own = 1.0 - ((a[0] + a[1]) + (a[2] + a[3]) + (a[4] + a[5]))
    fresh = []
    for f in range(FIELDS):
        near = [cut(behind[f]), cut(ahead[f])] + [cut(s) for s in shifted(q[f], lane)]
        terms = [w * n for w, n in zip(weights, near)]
        fresh.append(
            (own * cut(q[f]) + terms[0])
            + (terms[1] + terms[2])
            + (terms[3] + terms[4])
            + terms[5]
        )
    fresh[0] = fresh[0] + time_step * drag_rate * (vent_speed - cut(q[0]))
    fresh[2] = fresh[2] + time_step * buoyancy * cut(q[3])
    return fresh


def droplet(heat, soot, sprayed):
    kept = (1.0 - 0.5 * evap_rate) - 0.5 * evap_rate * jnp.tanh(0.5 * heat)
    heat = heat - latent_heat * (1.0 - kept) * sprayed
    soot = soot / (1.0 + scavenge * sprayed)
    return heat, soot, kept


def exchange_kernel(
    tun_size, sec_size, parts, detour,
    wind_hbm, heat_hbm, soot_hbm, mass_hbm, count_hbm, label_hbm, onset_hbm,
    state, fresh_mass, tally_out,
    ext, first, kept_first, spray_next, mass, count, label, onset, coef, mass_in, passing,
    pack_low, pack_high, from_low, from_high,
    local_sem, send_sem, recv_sem,
):
    X, Y, Z = heat_hbm.shape
    slots = mass_hbm.shape[0]
    t, s = lax.axis_index("tun"), lax.axis_index("sec")
    has = {-1: t > 0, 1: t < tun_size - 1}
    has_sec = {-1: s > 0, 1: s < sec_size - 1}

    def exists(dt, ds):
        if dt and ds:
            return jnp.logical_and(has[dt], has_sec[ds])
        return has[dt] if dt else has_sec[ds]

    around = [(a, b) for a in (-1, 0, 1) for b in (-1, 0, 1) if a or b]

    barrier = pltpu.get_barrier_semaphore()
    for a, b in around:
        @pl.when(exists(a, b))
        def _(a=a, b=b):
            pl.semaphore_signal(
                barrier, inc=1, device_id={"tun": t + a, "sec": s + b}, device_id_type=MESH
            )

    def load(i, src, dst):
        return pltpu.make_async_copy(src, dst, local_sem.at[i])

    loads = [
        load(0, wind_hbm, ext.at[0:3, 2:X + 2, 0:Y]),
        load(1, heat_hbm, ext.at[3, 2:X + 2, 0:Y]),
        load(2, soot_hbm, ext.at[4, 2:X + 2, 0:Y]),
        load(3, count_hbm, count),
        load(4, mass_hbm, mass),
        load(5, label_hbm, label),
        load(6, onset_hbm, onset),
    ]
    for c in loads:
        c.start()

    row = lax.broadcasted_iota(jnp.int32, (8, Z), 0)

    def pack(g):
        def one(x, _):
            low = high = None
            for j in range(4):
                f = 4 * g + j
                tile_low = ext[f, x + 2, 0:8]
                tile_high = ext[f, x + 2, Y - 8:Y]
                if j == 0:
                    low, high = tile_low, tile_high
                else:
                    here = jnp.logical_and(row >= 2 * j, row < 2 * j + 2)
                    low = jnp.where(here, pltpu.roll(tile_low, 2 * j, 0), low)
                    place = (2 * j + 6) % 8
                    there = jnp.logical_and(row >= place, row < place + 2)
                    high = jnp.where(there, pltpu.roll(tile_high, 2 * j, 0), high)
            pack_low[g, x] = low
            pack_high[g, x] = high
            return 0

        lax.fori_loop(0, X, one, 0, unroll=2)

    for at, to in ((0, 3), (3, 0), (3, 1), (1, 3)):
        @pl.when(t == detour + at)
        def _(distance=to - at):
            pl.semaphore_signal(
                barrier, inc=1, device_id={"tun": t + distance, "sec": s}, device_id_type=MESH
            )
    greeted = (
        (t == detour).astype(jnp.int32)
        + (t == detour + 1).astype(jnp.int32)
        + 2 * (t == detour + 3).astype(jnp.int32)
    )
    wide = has[-1].astype(jnp.int32) + has[1].astype(jnp.int32)
    deep = has_sec[-1].astype(jnp.int32) + has_sec[1].astype(jnp.int32)
    pl.semaphore_wait(barrier, (1 + wide) * (1 + deep) - 1 + greeted)

    def send(i, a, b, src, dst):
        return (a, b, pltpu.make_async_remote_copy(
            src_ref=src, dst_ref=dst, send_sem=send_sem.at[i], recv_sem=recv_sem.at[i],
            device_id={"tun": t + a, "sec": s + b}, device_id_type=MESH,
        ))

    def start(group):
        for a, b, copy in group:
            @pl.when(exists(a, b))
            def _(copy=copy):
                copy.start()

    def wait_recv(group):
        for a, b, copy in group:
            @pl.when(exists(-a, -b))
            def _(copy=copy):
                copy.wait_recv()

    fields = [
        send(0, 1, 0, wind_hbm.at[:, X - 2:X], ext.at[0:3, 0:2, 0:Y]),
        send(1, 1, 0, heat_hbm.at[X - 2:X], ext.at[3, 0:2, 0:Y]),
        send(2, 1, 0, soot_hbm.at[X - 2:X], ext.at[4, 0:2, 0:Y]),
        send(3, -1, 0, wind_hbm.at[:, 0:2], ext.at[0:3, X + 2:X + 4, 0:Y]),
        send(4, -1, 0, heat_hbm.at[0:2], ext.at[3, X + 2:X + 4, 0:Y]),
        send(5, -1, 0, soot_hbm.at[0:2], ext.at[4, X + 2:X + 4, 0:Y]),
    ]
    start(fields)

    for c in loads[:3]:
        c.wait()
    pack(0)
    rows_first = [
        send(8, 0, -1, pack_low.at[0], from_high.at[0, 1:X + 1]),
        send(9, 0, 1, pack_high.at[0], from_low.at[0, 1:X + 1]),
    ]
    start(rows_first)

    for c in loads[3:]:
        c.wait()

    def sums(x, _):
        n = count[x]
        terms = [jnp.where(n > k, mass[k, x], 0.0) for k in range(slots)]
        while len(terms) > 1:
            terms = [terms[i] + terms[i + 1] for i in range(0, len(terms) - 1, 2)] + (
                [terms[-1]] if len(terms) % 2 else [])
        zone = label[x]
        onset_here = jnp.full((Y, Z), 1 << 20, jnp.int32)
        for z in range(onset.shape[0]):
            onset_here = jnp.where(zone == z + 1, onset[z], onset_here)
        ext[LOAD, x + 2, 0:Y] = terms[0]
        ext[TALLY, x + 2, 0:Y] = n.astype(jnp.float32)
        ext[SPRAY, x + 2, 0:Y] = jnp.where(onset_here <= 0, inject_rate, 0.0)
        spray_next[x] = jnp.where(onset_here <= 1, inject_rate, 0.0)
        return 0

    lax.fori_loop(0, X, sums, 0, unroll=2)
    drops = [
        send(6, 1, 0, ext.at[LOAD:SPRAY, X:X + 2, 0:Y], ext.at[LOAD:SPRAY, 0:2, 0:Y]),
        send(7, 1, 0, ext.at[SPRAY, X + 1, 0:Y], ext.at[SPRAY, 1, 0:Y]),
        send(16, -1, 0, ext.at[SPRAY, 2, 0:Y], ext.at[SPRAY, X + 2, 0:Y]),
    ]
    start(drops)
    group = slots // parts
    masses = [
        send(17 + i, 1, 0, mass.at[i * group:(i + 1) * group, X - 2:X],
             mass_in.at[i * group:(i + 1) * group])
        for i in range(parts)
    ]
    start(masses[:1])

    def across_to(i, distance, src, dst):
        return pltpu.make_async_remote_copy(
            src_ref=src, dst_ref=dst, send_sem=send_sem.at[i], recv_sem=recv_sem.at[i],
            device_id={"tun": t + distance, "sec": s}, device_id_type=MESH,
        )

    outward = across_to(17 + parts, 3, mass.at[group:, X - 2:X], passing)
    onward = across_to(18 + parts, -2, passing, mass_in.at[group:])

    @pl.when(jnp.logical_and(has[1], t != detour))
    def _():
        masses[1][2].start()

    @pl.when(t == detour)
    def _():
        outward.start()

    pack(1)
    across = [
        send(10, 0, -1, pack_low.at[1], from_high.at[1, 1:X + 1]),
        send(11, 0, 1, pack_high.at[1], from_low.at[1, 1:X + 1]),
        send(12, -1, -1, pack_low.at[:, 0], from_high.at[:, X + 1]),
        send(13, 1, -1, pack_low.at[:, X - 1], from_high.at[:, 0]),
        send(14, -1, 1, pack_high.at[:, 0], from_low.at[:, X + 1]),
        send(15, 1, 1, pack_high.at[:, X - 1], from_low.at[:, 0]),
    ]
    start(across)

    @pl.when(jnp.logical_not(has[-1]))
    def _():
        ext[:, 0:2] = jnp.zeros((ALL, 2) + ext.shape[2:], jnp.float32)
        from_low[:, 0] = jnp.zeros((2, 8, Z), jnp.float32)
        from_high[:, 0] = jnp.zeros((2, 8, Z), jnp.float32)
        mass_in[...] = jnp.zeros(mass_in.shape, jnp.float32)

    @pl.when(jnp.logical_not(has[1]))
    def _():
        ext[:, X + 2:X + 4] = jnp.zeros((ALL, 2) + ext.shape[2:], jnp.float32)
        from_low[:, X + 1] = jnp.zeros((2, 8, Z), jnp.float32)
        from_high[:, X + 1] = jnp.zeros((2, 8, Z), jnp.float32)

    @pl.when(jnp.logical_not(has_sec[-1]))
    def _():
        from_low[...] = jnp.zeros(from_low.shape, jnp.float32)

    @pl.when(jnp.logical_not(has_sec[1]))
    def _():
        from_high[...] = jnp.zeros(from_high.shape, jnp.float32)

    wait_recv(rows_first + fields[3:] + drops[2:] + across[:2] + [across[2], across[4]])

    def unpacking(p, _):
        for g in range(2):
            high, low = from_high[g, p], from_low[g, p]
            for j in range(4):
                here = jnp.logical_and(row >= 2 * j, row < 2 * j + 2)
                tile = jnp.where(here, high, low)
                if j:
                    tile = pltpu.roll(tile, 8 - 2 * j, 0)
                ext[4 * g + j, p + 1, Y:Y + 8] = tile
        return 0

    lax.fori_loop(1, X + 2, unpacking, 0, unroll=3)

    lane = lax.broadcasted_iota(jnp.int32, (Y + 8, Z), 1)

    def substep_first(p, carry):
        th_behind, th = carry
        th_ahead = jnp.tanh(ext[3, p + 1])
        q = [ext[f, p] for f in range(FIELDS)]
        behind = [ext[f, p - 1] for f in range(FIELDS)]
        ahead = [ext[f, p + 1] for f in range(FIELDS)]
        fresh = transported(q, behind, ahead, th, th_behind, th_ahead, lane, Y + 8)
        sprayed = ext[LOAD, p - 1] + ext[SPRAY, p] * ext[TALLY, p - 1]
        fresh[3], fresh[4], kept = droplet(fresh[3], fresh[4], sprayed)
        for f in range(FIELDS):
            first[f, p - 1] = fresh[f]
        first[LOAD, p - 1] = kept * sprayed
        kept_first[p - 1] = kept[:Y]
        return th, th_ahead

    def first_planes(low, high):
        start_th = (jnp.tanh(ext[3, low - 1]), jnp.tanh(ext[3, low]))
        lax.fori_loop(low, high, substep_first, start_th, unroll=2)

        @pl.when(jnp.logical_not(has_sec[-1]))
        def _():
            first[:, low - 1:high - 1, Y + 7:Y + 8] = jnp.zeros(
                (FIELDS + 1, high - low, 1, Z), jnp.float32)

        @pl.when(jnp.logical_not(has_sec[1]))
        def _():
            first[:, low - 1:high - 1, Y:Y + 1] = jnp.zeros(
                (FIELDS + 1, high - low, 1, Z), jnp.float32)

    def substep_second(p, carry):
        th_behind, th = carry
        x = p - 1
        th_ahead = jnp.tanh(first[3, p + 1])
        q = [first[f, p] for f in range(FIELDS)]
        behind = [first[f, p - 1] for f in range(FIELDS)]
        ahead = [first[f, p + 1] for f in range(FIELDS)]
        fresh = transported(q, behind, ahead, th, th_behind, th_ahead, lane, Y)
        tally = ext[TALLY, x, 0:Y]
        spray = spray_next[x]
        sprayed = first[LOAD, p - 1, 0:Y] + spray * tally
        fresh[3], fresh[4], kept = droplet(fresh[3], fresh[4], sprayed)
        for f in range(FIELDS):
            state[f, x] = fresh[f]
        before = kept_first[p - 1]
        keep, add = before * kept, (ext[SPRAY, x + 1, 0:Y] * before + spray) * kept
        n = tally.astype(jnp.int32)
        tally_out[x] = n
        return keep, add, n, th, th_ahead

    def slot_masses(x, keep, add, n, source, plane, which=range(slots)):
        for k in which:
            m = source[k, plane]
            fresh_mass[k, x] = jnp.where(n > k, keep * m + add, m)

    def upper(p, carry):
        keep, add, n, th, th_ahead = substep_second(p, carry)
        slot_masses(p - 1, keep, add, n, mass, p - 3)
        return th, th_ahead

    def lowest(p, carry):
        keep, add, n, th, th_ahead = substep_second(p, carry)
        coef[0, p - 1], coef[1, p - 1] = keep, add
        return th, th_ahead

    first_planes(3, X + 3)

    @pl.when(t == detour + 3)
    def _():
        outward.wait_recv()
        onward.start()

    @pl.when(jnp.logical_not(has[1]))
    def _():
        first[:, X + 1] = jnp.zeros((FIELDS + 1, Y + 8, Z), jnp.float32)

    lax.fori_loop(3, X + 1, upper, (jnp.tanh(first[3, 2]), jnp.tanh(first[3, 3])), unroll=2)

    wait_recv(fields[:3] + drops[:2] + [across[3], across[5]])
    unpacking(0, 0)
    first_planes(1, 3)

    @pl.when(jnp.logical_not(has[-1]))
    def _():
        first[:, 0] = jnp.zeros((FIELDS + 1, Y + 8, Z), jnp.float32)

    lax.fori_loop(1, 3, lowest, (jnp.tanh(first[3, 0]), jnp.tanh(first[3, 1])), unroll=2)
    for i in range(parts):
        if i == 0:
            wait_recv(masses[:1])
        else:
            @pl.when(jnp.logical_and(has[-1], t != detour + 1))
            def _():
                masses[1][2].wait_recv()

            @pl.when(t == detour + 1)
            def _():
                onward.wait_recv()
        for x in range(2):
            slot_masses(x, coef[0, x], coef[1, x], tally_out[x], mass_in, x,
                        range(i * group, (i + 1) * group))
    for a, b, copy in rows_first + fields + drops + across + masses[:1]:
        @pl.when(exists(a, b))
        def _(copy=copy):
            copy.wait_send()

    @pl.when(jnp.logical_and(has[1], t != detour))
    def _():
        masses[1][2].wait_send()

    @pl.when(t == detour)
    def _():
        outward.wait_send()

    @pl.when(t == detour + 3)
    def _():
        onward.wait_send()


def output_kernel(state, mass, tally, wind_out, heat_out, soot_out, mass_out, count_out, sem):
    copies = [
        pltpu.make_async_copy(src, dst, sem.at[i])
        for i, (src, dst) in enumerate([
            (mass, mass_out),
            (state.at[0:3], wind_out),
            (state.at[3], heat_out),
            (state.at[4], soot_out),
            (tally, count_out),
        ])
    ]
    for c in copies:
        c.start()
    for c in copies:
        c.wait()


def local(tun_size, sec_size, wind, heat, soot, mass, count, label, onset):
    slots, X, Y, Z = mass.shape
    f32 = jnp.float32
    detour = 3 if tun_size == 8 else -8
    parts = 2
    any_spec = pl.BlockSpec(memory_space=pl.ANY)
    vmem_spec = pl.BlockSpec(memory_space=pltpu.VMEM)
    state, fresh_mass, tally = pl.pallas_call(
        functools.partial(exchange_kernel, tun_size, sec_size, parts, detour),
        out_shape=(
            jax.ShapeDtypeStruct((FIELDS, X, Y, Z), f32),
            jax.ShapeDtypeStruct((slots, X, Y, Z), f32),
            jax.ShapeDtypeStruct((X, Y, Z), jnp.int32),
        ),
        in_specs=[pl.BlockSpec(memory_space=pltpu.HBM)] * 7,
        out_specs=(vmem_spec,) * 3,
        scratch_shapes=[
            pltpu.VMEM((ALL, X + 4, Y + 8, Z), f32),
            pltpu.VMEM((FIELDS + 1, X + 2, Y + 8, Z), f32),
            pltpu.VMEM((X + 2, Y, Z), f32),
            pltpu.VMEM((X, Y, Z), f32),
            pltpu.VMEM((slots, X, Y, Z), f32),
            pltpu.VMEM((X, Y, Z), jnp.int32),
            pltpu.VMEM((X, Y, Z), jnp.int32),
            pltpu.SMEM(onset.shape, jnp.int32),
            pltpu.VMEM((2, 2, Y, Z), f32),
            pltpu.VMEM((slots, 2, Y, Z), f32),
            pltpu.VMEM((slots // 2, 2, Y, Z), f32),
            pltpu.VMEM((2, X, 8, Z), f32),
            pltpu.VMEM((2, X, 8, Z), f32),
            pltpu.VMEM((2, X + 2, 8, Z), f32),
            pltpu.VMEM((2, X + 2, 8, Z), f32),
            pltpu.SemaphoreType.DMA((7,)),
            pltpu.SemaphoreType.DMA((19 + parts,)),
            pltpu.SemaphoreType.DMA((19 + parts,)),
        ],
        compiler_params=pltpu.CompilerParams(
            collective_id=0, has_side_effects=True, vmem_limit_bytes=24 << 20
        ),
        name="fields",
    )(*[
        pltpu.with_memory_space_constraint(a, pltpu.HBM)
        for a in (wind, heat, soot, mass, count, label, onset)
    ])
    return pl.pallas_call(
        output_kernel,
        out_shape=(
            jax.ShapeDtypeStruct((3, X, Y, Z), f32),
            jax.ShapeDtypeStruct((X, Y, Z), f32),
            jax.ShapeDtypeStruct((X, Y, Z), f32),
            jax.ShapeDtypeStruct((slots, X, Y, Z), f32),
            jax.ShapeDtypeStruct((X, Y, Z), jnp.int32),
        ),
        in_specs=[vmem_spec] * 3,
        out_specs=(any_spec,) * 5,
        scratch_shapes=[pltpu.SemaphoreType.DMA((5,))],
        compiler_params=pltpu.CompilerParams(vmem_limit_bytes=24 << 20),
        name="outputs",
    )(state, fresh_mass, tally)


def solution(mesh):
    return jax.shard_map(
        functools.partial(local, mesh.shape["tun"], mesh.shape["sec"]),
        mesh=mesh,
        in_specs=(
            P(None, "tun", "sec", None),
            P("tun", "sec", None),
            P("tun", "sec", None),
            P(None, "tun", "sec", None),
            P("tun", "sec", None),
            P("tun", "sec", None),
            P(),
        ),
        out_specs=(
            P(None, "tun", "sec", None),
            P("tun", "sec", None),
            P("tun", "sec", None),
            P(None, "tun", "sec", None),
            P("tun", "sec", None),
        ),
        check_vma=False,
    )
```

```python
import functools

import jax
import jax.numpy as jnp
from jax import lax
from jax.experimental import pallas as pl
from jax.experimental.pallas import tpu as pltpu
from jax.sharding import PartitionSpec as P

visc_base = 0.2
time_step = 0.1
buoyancy = 0.5
drag_rate = 0.3
vent_speed = 1.0
inject_rate = 0.5
evap_rate = 0.4
latent_heat = 0.5
scavenge = 0.3

MESH = pl.DeviceIdType.MESH
FIELDS = 5
LOAD, TALLY, SPRAY = 5, 6, 7
ALL = 8


def shifted(c, lane):
    rows, depth = c.shape
    below = pltpu.roll(c, 1, 0)
    above = pltpu.roll(c, rows - 1, 0)
    down = jnp.where(lane == 0, 0.0, pltpu.roll(c, 1, 1))
    up = jnp.where(lane == depth - 1, 0.0, pltpu.roll(c, depth - 1, 1))
    return below, above, down, up


def transported(q, behind, ahead, th, th_behind, th_ahead, lane, keep):
    cut = lambda a: a[:keep]
    around_th = [cut(a) for a in shifted(th, lane)]
    th0 = cut(th)
    half = 0.5 * time_step
    base = 2.0 * visc_base * half
    slope = 0.5 * visc_base * half
    mine = base + slope * th0
    wind = [half * cut(q[d]) for d in range(3)]
    a = [mine + slope * t for t in [cut(th_behind), cut(th_ahead)] + around_th]
    weights = [
        a[0] + wind[0], a[1] - wind[0],
        a[2] + wind[1], a[3] - wind[1],
        a[4] + wind[2], a[5] - wind[2],
    ]
    own = 1.0 - ((a[0] + a[1]) + (a[2] + a[3]) + (a[4] + a[5]))
    fresh = []
    for f in range(FIELDS):
        near = [cut(behind[f]), cut(ahead[f])] + [cut(s) for s in shifted(q[f], lane)]
        terms = [w * n for w, n in zip(weights, near)]
        fresh.append(
            (own * cut(q[f]) + terms[0])
            + (terms[1] + terms[2])
            + (terms[3] + terms[4])
            + terms[5]
        )
    fresh[0] = fresh[0] + time_step * drag_rate * (vent_speed - cut(q[0]))
    fresh[2] = fresh[2] + time_step * buoyancy * cut(q[3])
    return fresh


def droplet(heat, soot, sprayed):
    kept = (1.0 - 0.5 * evap_rate) - 0.5 * evap_rate * jnp.tanh(0.5 * heat)
    heat = heat - latent_heat * (1.0 - kept) * sprayed
    soot = soot / (1.0 + scavenge * sprayed)
    return heat, soot, kept


def exchange_kernel(
    tun_size, sec_size, parts,
    wind_hbm, heat_hbm, soot_hbm, mass_hbm, count_hbm, label_hbm, onset_hbm,
    state, fresh_mass, tally_out,
    ext, first, kept_first, spray_next, mass, count, label, onset, coef, mass_in,
    pack_low, pack_high, from_low, from_high,
    local_sem, send_sem, recv_sem,
):
    X, Y, Z = heat_hbm.shape
    slots = mass_hbm.shape[0]
    t, s = lax.axis_index("tun"), lax.axis_index("sec")
    has = {-1: t > 0, 1: t < tun_size - 1}
    has_sec = {-1: s > 0, 1: s < sec_size - 1}

    def exists(dt, ds):
        if dt and ds:
            return jnp.logical_and(has[dt], has_sec[ds])
        return has[dt] if dt else has_sec[ds]

    around = [(a, b) for a in (-1, 0, 1) for b in (-1, 0, 1) if a or b]

    barrier = pltpu.get_barrier_semaphore()
    for a, b in around:
        @pl.when(exists(a, b))
        def _(a=a, b=b):
            pl.semaphore_signal(
                barrier, inc=1, device_id={"tun": t + a, "sec": s + b}, device_id_type=MESH
            )

    def load(i, src, dst):
        return pltpu.make_async_copy(src, dst, local_sem.at[i])

    loads = [
        load(0, wind_hbm, ext.at[0:3, 2:X + 2, 0:Y]),
        load(1, heat_hbm, ext.at[3, 2:X + 2, 0:Y]),
        load(2, soot_hbm, ext.at[4, 2:X + 2, 0:Y]),
        load(3, count_hbm, count),
        load(4, mass_hbm, mass),
        load(5, label_hbm, label),
        load(6, onset_hbm, onset),
    ]
    for c in loads:
        c.start()

    row = lax.broadcasted_iota(jnp.int32, (8, Z), 0)

    def pack(g):
        def one(x, _):
            low = high = None
            for j in range(4):
                f = 4 * g + j
                tile_low = ext[f, x + 2, 0:8]
                tile_high = ext[f, x + 2, Y - 8:Y]
                if j == 0:
                    low, high = tile_low, tile_high
                else:
                    here = jnp.logical_and(row >= 2 * j, row < 2 * j + 2)
                    low = jnp.where(here, pltpu.roll(tile_low, 2 * j, 0), low)
                    place = (2 * j + 6) % 8
                    there = jnp.logical_and(row >= place, row < place + 2)
                    high = jnp.where(there, pltpu.roll(tile_high, 2 * j, 0), high)
            pack_low[g, x] = low
            pack_high[g, x] = high
            return 0

        lax.fori_loop(0, X, one, 0, unroll=2)

    wide = has[-1].astype(jnp.int32) + has[1].astype(jnp.int32)
    deep = has_sec[-1].astype(jnp.int32) + has_sec[1].astype(jnp.int32)
    pl.semaphore_wait(barrier, (1 + wide) * (1 + deep) - 1)

    def send(i, a, b, src, dst):
        return (a, b, pltpu.make_async_remote_copy(
            src_ref=src, dst_ref=dst, send_sem=send_sem.at[i], recv_sem=recv_sem.at[i],
            device_id={"tun": t + a, "sec": s + b}, device_id_type=MESH,
        ))

    def start(group):
        for a, b, copy in group:
            @pl.when(exists(a, b))
            def _(copy=copy):
                copy.start()

    def wait_recv(group):
        for a, b, copy in group:
            @pl.when(exists(-a, -b))
            def _(copy=copy):
                copy.wait_recv()

    fields = [
        send(0, 1, 0, wind_hbm.at[:, X - 2:X], ext.at[0:3, 0:2, 0:Y]),
        send(1, 1, 0, heat_hbm.at[X - 2:X], ext.at[3, 0:2, 0:Y]),
        send(2, 1, 0, soot_hbm.at[X - 2:X], ext.at[4, 0:2, 0:Y]),
        send(3, -1, 0, wind_hbm.at[:, 0:2], ext.at[0:3, X + 2:X + 4, 0:Y]),
        send(4, -1, 0, heat_hbm.at[0:2], ext.at[3, X + 2:X + 4, 0:Y]),
        send(5, -1, 0, soot_hbm.at[0:2], ext.at[4, X + 2:X + 4, 0:Y]),
    ]
    start(fields)
    group = slots // parts
    masses = [
        send(17 + i, 1, 0, mass_hbm.at[i * group:(i + 1) * group, X - 2:X],
             mass_in.at[i * group:(i + 1) * group])
        for i in range(parts)
    ]
    start(masses[:1])

    for c in loads[:3]:
        c.wait()
    pack(0)
    rows_first = [
        send(8, 0, -1, pack_low.at[0], from_high.at[0, 1:X + 1]),
        send(9, 0, 1, pack_high.at[0], from_low.at[0, 1:X + 1]),
    ]
    start(rows_first)

    for c in loads[3:]:
        c.wait()

    def sums(x, _):
        n = count[x]
        terms = [jnp.where(n > k, mass[k, x], 0.0) for k in range(slots)]
        while len(terms) > 1:
            terms = [terms[i] + terms[i + 1] for i in range(0, len(terms) - 1, 2)] + (
                [terms[-1]] if len(terms) % 2 else [])
        zone = label[x]
        onset_here = jnp.full((Y, Z), 1 << 20, jnp.int32)
        for z in range(onset.shape[0]):
            onset_here = jnp.where(zone == z + 1, onset[z], onset_here)
        ext[LOAD, x + 2, 0:Y] = terms[0]
        ext[TALLY, x + 2, 0:Y] = n.astype(jnp.float32)
        ext[SPRAY, x + 2, 0:Y] = jnp.where(onset_here <= 0, inject_rate, 0.0)
        spray_next[x] = jnp.where(onset_here <= 1, inject_rate, 0.0)
        return 0

    lax.fori_loop(0, X, sums, 0, unroll=2)
    drops = [
        send(6, 1, 0, ext.at[LOAD:SPRAY, X:X + 2, 0:Y], ext.at[LOAD:SPRAY, 0:2, 0:Y]),
        send(7, 1, 0, ext.at[SPRAY, X + 1, 0:Y], ext.at[SPRAY, 1, 0:Y]),
        send(16, -1, 0, ext.at[SPRAY, 2, 0:Y], ext.at[SPRAY, X + 2, 0:Y]),
    ]
    start(drops)
    start(masses[1:])

    pack(1)
    across = [
        send(10, 0, -1, pack_low.at[1], from_high.at[1, 1:X + 1]),
        send(11, 0, 1, pack_high.at[1], from_low.at[1, 1:X + 1]),
        send(12, -1, -1, pack_low.at[:, 0], from_high.at[:, X + 1]),
        send(13, 1, -1, pack_low.at[:, X - 1], from_high.at[:, 0]),
        send(14, -1, 1, pack_high.at[:, 0], from_low.at[:, X + 1]),
        send(15, 1, 1, pack_high.at[:, X - 1], from_low.at[:, 0]),
    ]
    start(across)

    @pl.when(jnp.logical_not(has[-1]))
    def _():
        ext[:, 0:2] = jnp.zeros((ALL, 2) + ext.shape[2:], jnp.float32)
        from_low[:, 0] = jnp.zeros((2, 8, Z), jnp.float32)
        from_high[:, 0] = jnp.zeros((2, 8, Z), jnp.float32)
        mass_in[...] = jnp.zeros(mass_in.shape, jnp.float32)

    @pl.when(jnp.logical_not(has[1]))
    def _():
        ext[:, X + 2:X + 4] = jnp.zeros((ALL, 2) + ext.shape[2:], jnp.float32)
        from_low[:, X + 1] = jnp.zeros((2, 8, Z), jnp.float32)
        from_high[:, X + 1] = jnp.zeros((2, 8, Z), jnp.float32)

    @pl.when(jnp.logical_not(has_sec[-1]))
    def _():
        from_low[...] = jnp.zeros(from_low.shape, jnp.float32)

    @pl.when(jnp.logical_not(has_sec[1]))
    def _():
        from_high[...] = jnp.zeros(from_high.shape, jnp.float32)

    wait_recv(rows_first + fields[3:] + drops[2:] + across[:2] + [across[2], across[4]])

    def unpacking(p, _):
        for g in range(2):
            high, low = from_high[g, p], from_low[g, p]
            for j in range(4):
                here = jnp.logical_and(row >= 2 * j, row < 2 * j + 2)
                tile = jnp.where(here, high, low)
                if j:
                    tile = pltpu.roll(tile, 8 - 2 * j, 0)
                ext[4 * g + j, p + 1, Y:Y + 8] = tile
        return 0

    lax.fori_loop(1, X + 2, unpacking, 0, unroll=3)

    lane = lax.broadcasted_iota(jnp.int32, (Y + 8, Z), 1)

    def substep_first(p, carry):
        th_behind, th = carry
        th_ahead = jnp.tanh(ext[3, p + 1])
        q = [ext[f, p] for f in range(FIELDS)]
        behind = [ext[f, p - 1] for f in range(FIELDS)]
        ahead = [ext[f, p + 1] for f in range(FIELDS)]
        fresh = transported(q, behind, ahead, th, th_behind, th_ahead, lane, Y + 8)
        sprayed = ext[LOAD, p - 1] + ext[SPRAY, p] * ext[TALLY, p - 1]
        fresh[3], fresh[4], kept = droplet(fresh[3], fresh[4], sprayed)
        for f in range(FIELDS):
            first[f, p - 1] = fresh[f]
        first[LOAD, p - 1] = kept * sprayed
        kept_first[p - 1] = kept[:Y]
        return th, th_ahead

    def first_planes(low, high):
        start_th = (jnp.tanh(ext[3, low - 1]), jnp.tanh(ext[3, low]))
        lax.fori_loop(low, high, substep_first, start_th, unroll=2)

        @pl.when(jnp.logical_not(has_sec[-1]))
        def _():
            first[:, low - 1:high - 1, Y + 7:Y + 8] = jnp.zeros(
                (FIELDS + 1, high - low, 1, Z), jnp.float32)

        @pl.when(jnp.logical_not(has_sec[1]))
        def _():
            first[:, low - 1:high - 1, Y:Y + 1] = jnp.zeros(
                (FIELDS + 1, high - low, 1, Z), jnp.float32)

    def substep_second(p, carry):
        th_behind, th = carry
        x = p - 1
        th_ahead = jnp.tanh(first[3, p + 1])
        q = [first[f, p] for f in range(FIELDS)]
        behind = [first[f, p - 1] for f in range(FIELDS)]
        ahead = [first[f, p + 1] for f in range(FIELDS)]
        fresh = transported(q, behind, ahead, th, th_behind, th_ahead, lane, Y)
        tally = ext[TALLY, x, 0:Y]
        spray = spray_next[x]
        sprayed = first[LOAD, p - 1, 0:Y] + spray * tally
        fresh[3], fresh[4], kept = droplet(fresh[3], fresh[4], sprayed)
        for f in range(FIELDS):
            state[f, x] = fresh[f]
        before = kept_first[p - 1]
        keep, add = before * kept, (ext[SPRAY, x + 1, 0:Y] * before + spray) * kept
        n = tally.astype(jnp.int32)
        tally_out[x] = n
        return keep, add, n, th, th_ahead

    def slot_masses(x, keep, add, n, source, plane, which=range(slots)):
        for k in which:
            m = source[k, plane]
            fresh_mass[k, x] = jnp.where(n > k, keep * m + add, m)

    def upper(p, carry):
        keep, add, n, th, th_ahead = substep_second(p, carry)
        slot_masses(p - 1, keep, add, n, mass, p - 3)
        return th, th_ahead

    def lowest(p, carry):
        keep, add, n, th, th_ahead = substep_second(p, carry)
        coef[0, p - 1], coef[1, p - 1] = keep, add
        return th, th_ahead

    first_planes(3, X + 3)

    @pl.when(jnp.logical_not(has[1]))
    def _():
        first[:, X + 1] = jnp.zeros((FIELDS + 1, Y + 8, Z), jnp.float32)

    lax.fori_loop(3, X + 1, upper, (jnp.tanh(first[3, 2]), jnp.tanh(first[3, 3])), unroll=2)

    wait_recv(fields[:3] + drops[:2] + [across[3], across[5]])
    unpacking(0, 0)
    first_planes(1, 3)

    @pl.when(jnp.logical_not(has[-1]))
    def _():
        first[:, 0] = jnp.zeros((FIELDS + 1, Y + 8, Z), jnp.float32)

    lax.fori_loop(1, 3, lowest, (jnp.tanh(first[3, 0]), jnp.tanh(first[3, 1])), unroll=2)
    for i in range(parts):
        wait_recv(masses[i:i + 1])
        for x in range(2):
            slot_masses(x, coef[0, x], coef[1, x], tally_out[x], mass_in, x,
                        range(i * group, (i + 1) * group))
    for a, b, copy in rows_first + fields + drops + across + masses:
        @pl.when(exists(a, b))
        def _(copy=copy):
            copy.wait_send()


def output_kernel(state, mass, tally, wind_out, heat_out, soot_out, mass_out, count_out, sem):
    copies = [
        pltpu.make_async_copy(src, dst, sem.at[i])
        for i, (src, dst) in enumerate([
            (mass, mass_out),
            (state.at[0:3], wind_out),
            (state.at[3], heat_out),
            (state.at[4], soot_out),
            (tally, count_out),
        ])
    ]
    for c in copies:
        c.start()
    for c in copies:
        c.wait()


def local(tun_size, sec_size, wind, heat, soot, mass, count, label, onset):
    slots, X, Y, Z = mass.shape
    f32 = jnp.float32
    parts = 4 if slots % 4 == 0 else 1
    any_spec = pl.BlockSpec(memory_space=pl.ANY)
    vmem_spec = pl.BlockSpec(memory_space=pltpu.VMEM)
    state, fresh_mass, tally = pl.pallas_call(
        functools.partial(exchange_kernel, tun_size, sec_size, parts),
        out_shape=(
            jax.ShapeDtypeStruct((FIELDS, X, Y, Z), f32),
            jax.ShapeDtypeStruct((slots, X, Y, Z), f32),
            jax.ShapeDtypeStruct((X, Y, Z), jnp.int32),
        ),
        in_specs=[pl.BlockSpec(memory_space=pltpu.HBM)] * 7,
        out_specs=(vmem_spec,) * 3,
        scratch_shapes=[
            pltpu.VMEM((ALL, X + 4, Y + 8, Z), f32),
            pltpu.VMEM((FIELDS + 1, X + 2, Y + 8, Z), f32),
            pltpu.VMEM((X + 2, Y, Z), f32),
            pltpu.VMEM((X, Y, Z), f32),
            pltpu.VMEM((slots, X, Y, Z), f32),
            pltpu.VMEM((X, Y, Z), jnp.int32),
            pltpu.VMEM((X, Y, Z), jnp.int32),
            pltpu.SMEM(onset.shape, jnp.int32),
            pltpu.VMEM((2, 2, Y, Z), f32),
            pltpu.VMEM((slots, 2, Y, Z), f32),
            pltpu.VMEM((2, X, 8, Z), f32),
            pltpu.VMEM((2, X, 8, Z), f32),
            pltpu.VMEM((2, X + 2, 8, Z), f32),
            pltpu.VMEM((2, X + 2, 8, Z), f32),
            pltpu.SemaphoreType.DMA((7,)),
            pltpu.SemaphoreType.DMA((17 + parts,)),
            pltpu.SemaphoreType.DMA((17 + parts,)),
        ],
        compiler_params=pltpu.CompilerParams(
            collective_id=0, has_side_effects=True, vmem_limit_bytes=24 << 20
        ),
        name="fields",
    )(*[
        pltpu.with_memory_space_constraint(a, pltpu.HBM)
        for a in (wind, heat, soot, mass, count, label, onset)
    ])
    return pl.pallas_call(
        output_kernel,
        out_shape=(
            jax.ShapeDtypeStruct((3, X, Y, Z), f32),
            jax.ShapeDtypeStruct((X, Y, Z), f32),
            jax.ShapeDtypeStruct((X, Y, Z), f32),
            jax.ShapeDtypeStruct((slots, X, Y, Z), f32),
            jax.ShapeDtypeStruct((X, Y, Z), jnp.int32),
        ),
        in_specs=[vmem_spec] * 3,
        out_specs=(any_spec,) * 5,
        scratch_shapes=[pltpu.SemaphoreType.DMA((5,))],
        compiler_params=pltpu.CompilerParams(vmem_limit_bytes=24 << 20),
        name="outputs",
    )(state, fresh_mass, tally)


def solution(mesh):
    return jax.shard_map(
        functools.partial(local, mesh.shape["tun"], mesh.shape["sec"]),
        mesh=mesh,
        in_specs=(
            P(None, "tun", "sec", None),
            P("tun", "sec", None),
            P("tun", "sec", None),
            P(None, "tun", "sec", None),
            P("tun", "sec", None),
            P("tun", "sec", None),
            P(),
        ),
        out_specs=(
            P(None, "tun", "sec", None),
            P("tun", "sec", None),
            P("tun", "sec", None),
            P(None, "tun", "sec", None),
            P("tun", "sec", None),
        ),
        check_vma=False,
    )
```
